512 devices in a mesh: lag: 64 (over z, x_hi, core), out: 8 (over x_lo, y).
Axes of the slice: x: 4 (x_hi: 2, x_lo: 2; x = x_hi * 2 + x_lo), y: 4, z: 16, core: 2. Of those that a mesh axis runs over, the one named last changes fastest.
Arguments:
- markov: float32 [2048, 256, 64], P('lag', 'out'), may hold values from -6 to 6
- basis: float32 [2048, 512], P('lag'), may hold values from -0.125 to 0.125
Outputs:
- reduced: float32 [64, 2, 512, 512], P('lag', None, 'out')
The draws below stay inside these ranges and needn't reach their ends.
All inputs are finite; a program needn't handle non-finite values.
Results may differ from the reference program's by a relative error of at most 0.0003.
Values sent between devices are 32-bit elements; how exact they have to be, the bound alone decides.
A program may use at most 128 MiB of HBM per device.

```python
import jax
import jax.numpy as jnp
from jax import lax

P_SIZE = 256
M = 64
R = 512
S = 32
LAG_DEV = 32
LAGS = 2048
N_LAG = 64


def level_of(stream_key, shape, shards, least, largest):
    level = 1.0
    for position, parts in shards:
        heights = jax.random.uniform(jax.random.fold_in(jax.random.fold_in(stream_key, 6), position), (parts,), jnp.float32, least / len(shards), largest / len(shards))
        level = level * jnp.repeat(jnp.exp(heights), shape[position] // parts).reshape((-1,) + (1,) * (len(shape) - 1 - position))
    return level


def noise(rng, shape, scale, bound, shards=(), kind=jnp.bfloat16):
    drawn = scale * jax.random.normal(rng, shape, jnp.float32)
    if shards:
        drawn = drawn * level_of(rng, shape, shards, -0.22, 0.18)
    return jnp.clip(drawn, -bound, bound).astype(kind)


def setup_inputs(seed: int = 0) -> dict:
    seeds = jax.random.split(jax.random.key(seed), 3)
    return {
        "markov": noise(seeds[0], (LAGS, P_SIZE, M), 1.0, 6.0, ((0, 64), (1, 8)), jnp.float32),
        "basis": noise(seeds[1], (S * M, R), (S * M) ** -0.5, 0.125, ((0, 64),), jnp.float32),
    }


def block_grams(padded, basis, index):
    start = (index * LAG_DEV).astype(jnp.int32)
    window = lax.dynamic_slice_in_dim(padded, start, LAG_DEV + S, 0)
    slabs = [window[j:j + LAG_DEV + 1] for j in range(S)]
    hankel = jnp.stack(slabs, axis=2).reshape((LAG_DEV + 1) * P_SIZE, S * M)
    projected = jnp.dot(hankel, basis, preferred_element_type=jnp.float32, precision=lax.Precision.HIGHEST)
    early = projected[:LAG_DEV * P_SIZE]
    later = projected[P_SIZE:]
    dims = (((0,), (0,)), ((), ()))
    first = lax.dot_general(early, early, dims, precision=lax.Precision.HIGHEST)
    second = lax.dot_general(early, later, dims, precision=lax.Precision.HIGHEST)
    return jnp.stack([first, second])


def reference(markov, basis):
    padded = jnp.concatenate([markov, jnp.zeros((S, P_SIZE, M), markov.dtype)], axis=0)
    grams = lax.map(lambda index: block_grams(padded, basis, index), jnp.arange(N_LAG, dtype=jnp.int32))
    totals = jnp.cumsum(grams, axis=0)
    counts = (jnp.arange(1, N_LAG + 1) * (LAG_DEV * P_SIZE)).astype(grams.dtype)
    return totals / counts[:, None, None, None]
```

```python
import jax
import jax.numpy as jnp
from jax import lax
from jax.experimental import pallas as pl
from jax.experimental.pallas import tpu as pltpu
from jax.sharding import PartitionSpec as P

P_SIZE = 256
LAG_DEV = 32
MESH = pl.DeviceIdType.MESH
F32 = jnp.float32
BF16 = jnp.bfloat16

NZ = 16
CHUNKS = 4
ROWS = 1056
TILE_M = 528


def split(value):
    high = value.astype(BF16)
    low = (value - high.astype(F32)).astype(BF16)
    return high, low


def device(x, y, z, core):
    return (4 * z + 2 * lax.div(x, 2) + core, 4 * lax.rem(x, 2) + y)


def dot(a, b):
    return jnp.dot(a, b, preferred_element_type=F32)


def kernel(
    markov, basis, out,
    packed, pairs, lhs, gathered, weights, proj, right_hi, right_lo, left_hi, left_lo,
    gram_out, gram_in, gram, plane, states, tiles_out, tiles_in, before_out, before_in, final,
    mk_s, mk_r, b1_s, b1_r, b2_s, b2_r, b3_s, b3_r, b4_s, b4_r, cs_s, cs_r, pl_s, pl_r,
    e1_s, e1_r, e2_s, e2_r, f_s, f_r,
):
    lag = lax.axis_index("lag")
    chan = lax.axis_index("out")
    z = lax.div(lag, 4)
    x_hi = lax.rem(lax.div(lag, 2), 2)
    core = lax.rem(lag, 2)
    x_lo = lax.div(chan, 4)
    y = lax.rem(chan, 4)
    x = 2 * x_hi + x_lo
    block = 4 * z + x
    swapped = core != x_lo

    def remote(src, dst, send, recv, to):
        return pltpu.make_async_remote_copy(
            src_ref=src, dst_ref=dst, send_sem=send, recv_sem=recv, device_id=to, device_id_type=MESH
        )

    def around(value, step, size):
        return lax.rem(value + step, size)

    barrier = pltpu.get_barrier_semaphore()

    def greet(to):
        pl.semaphore_signal(barrier, inc=1, device_id=to, device_id_type=MESH)

    @pl.loop(1, NZ)
    def _(d):
        greet(device(x, y, around(z, d, NZ), core))

    @pl.loop(1, 16)
    def _(d):
        greet(device(around(x, lax.div(d, 4), 4), around(y, lax.rem(d, 4), 4), z, core))

    @pl.loop(0, 4)
    def _(d):
        greet(device(around(x, d, 4), y, z, 1 - core))

    gives_down = jnp.logical_and(lax.rem(lag, 4) == 0, z > 0)
    takes_up = jnp.logical_and(x == 3, z < NZ - 1)

    @pl.when(gives_down)
    def _():
        greet(device(3, y, z - 1, x_lo))

    @pl.when(takes_up)
    def _():
        greet((4 * (z + 1), 4 * core + y))

    for t in range(LAG_DEV // 2):
        packed[t] = jnp.concatenate([markov[2 * t], markov[2 * t + 1]], axis=-1)

    rows8 = pl.ds(pl.multiple_of(8 * y, 8), 8)
    cols = pl.ds(pl.multiple_of(256 * x_lo, 256), 256)
    gathered[z, x_hi, core, y, :, cols] = basis[rows8, cols]

    pl.semaphore_wait(barrier, 34 + gives_down.astype(jnp.int32) + takes_up.astype(jnp.int32))

    def level1(d, zz):
        piece = gathered.at[zz, x_hi, core, y, :, cols]
        return remote(piece, piece, b1_s.at[d - 1], b1_r.at[d - 1], device(x, y, around(z, d, NZ), core))

    @pl.loop(1, NZ)
    def _(d):
        level1(d, z).start()

    def to_block():
        return remote(packed, pairs.at[0], mk_s.at[0], mk_r.at[0], device(2 * x_hi + core, y, z, x_lo))

    def to_before():
        earlier = lag - 1
        to = device(lax.rem(earlier, 4), y, lax.div(earlier, 4), x_lo)
        return remote(packed, pairs.at[1], mk_s.at[1], mk_r.at[1], to)

    @pl.when(swapped)
    def _():
        to_block().start()

    @pl.when(lag > 0)
    def _():
        to_before().start()

    @pl.when(jnp.logical_not(swapped))
    def _():
        pairs[0] = packed[...]

    @pl.when(block == 4 * NZ - 1)
    def _():
        pairs[1] = jnp.zeros_like(packed)

    def chunk_of(q):
        return lax.rem(lax.div(z, 4) + q, CHUNKS)

    def zs_of(q):
        return pl.ds(4 * chunk_of(q), 4)

    def wait_level1(q):
        @pl.loop(0, 4)
        def _(i):
            source = 4 * chunk_of(q) + i
            d = lax.rem(z - source + NZ, NZ)

            @pl.when(d > 0)
            def _():
                level1(d, source).wait_recv()

    def level2(q, d):
        piece = gathered.at[zs_of(q), x_hi, core, y, :, cols]
        along_y = core == 0
        to = device(
            jnp.where(along_y, x, around(x, d, 4)), jnp.where(along_y, around(y, d, 4), y), z, core
        )
        slot = 3 * q + d - 1
        return remote(piece, piece, b2_s.at[slot], b2_r.at[slot], to)

    def level3(q, d, which):
        slot = 3 * q + d - 1
        if which == 0:
            piece = gathered.at[zs_of(q), x_hi, 0, :, :, cols]
            to = device(around(x, d, 4), y, z, 0)
        else:
            piece = gathered.at[zs_of(q), :, 1, y]
            to = device(x, around(y, d, 4), z, 1)
        return remote(piece, piece, b3_s.at[slot], b3_r.at[slot], to)

    def by_core(act):
        for which in (0, 1):
            @pl.when(core == which)
            def _():
                act(which)

    def level4(q):
        piece = gathered.at[zs_of(q), :, core]
        return remote(piece, piece, b4_s.at[q], b4_r.at[q], device(x, y, z, 1 - core))

    def wait2_start3(q):
        for d in (1, 2, 3):
            level2(q, d).wait_recv()

        def act(which):
            for d in (1, 2, 3):
                level3(q, d, which).start()

        by_core(act)

    def wait3_start4(q):
        def act(which):
            for d in (1, 2, 3):
                level3(q, d, which).wait_recv()

        by_core(act)
        level4(q).start()

    def wait1_start2(q):
        wait_level1(q)
        for d in (1, 2, 3):
            level2(q, d).start()

    def build_lhs():
        @pl.when(swapped)
        def _():
            to_block().wait_recv()

        @pl.when(block < 4 * NZ - 1)
        def _():
            to_before().wait_recv()

        first_half = lax.broadcasted_iota(jnp.int32, (32, 128), 1) < 64

        def put(t, value):
            high, low = split(value)
            for place, part in ((0, high), (256, low), (512, high)):
                lhs[pl.ds(pl.multiple_of(32 * t + 64, 32), 32), place : place + 128] = part
                lhs[pl.ds(pl.multiple_of(32 * t, 32), 32), place + 128 : place + 256] = part

        def both(t, this, following):
            put(2 * t, this)
            put(2 * t + 1, jnp.where(first_half, pltpu.roll(this, 64, 1), pltpu.roll(following, 64, 1)))

        for side in (0, 1):
            @pl.loop(0, 15)
            def _(t):
                both(16 * side + t, pairs[side, t], pairs[side, t + 1])

        both(15, pairs[0, 15], pairs[1, 0])
        put(62, pairs[1, 15])

    def compute(q):
        level4(q).wait_recv()

        @pl.loop(0, 2)
        def _(k):
            part = 2 * chunk_of(q) + k
            for i in range(2):
                for h in range(2):
                    for w in range(2):
                        high, low = split(gathered[2 * part + i, h, w].reshape(32, 512))
                        at = 128 * i + 64 * h + 32 * w
                        weights[at : at + 32, :] = high
                        weights[256 + at : 288 + at, :] = high
                        weights[512 + at : 544 + at, :] = low

            @pl.loop(0, ROWS // TILE_M)
            def _(m):
                here = pl.ds(pl.multiple_of(TILE_M * m, 16), TILE_M)
                there = pl.ds(pl.multiple_of(128 * part + 64 + TILE_M * m, 16), TILE_M)
                proj[here, :] += dot(lhs[there, :], weights[...])

    wait1_start2(0)
    build_lhs()
    proj[...] = jnp.zeros_like(proj)
    for step in range(1, CHUNKS + 3):
        if 0 <= step - 1 < CHUNKS:
            wait2_start3(step - 1)
        if 0 <= step - 2 < CHUNKS:
            wait3_start4(step - 2)
        if step < CHUNKS:
            wait1_start2(step)
        if 0 <= step - 3 < CHUNKS:
            compute(step - 3)

    @pl.loop(0, 8)
    def _(i):
        here = pl.ds(pl.multiple_of(128 * i, 128), 128)
        value = proj[here, :]
        high, low = split(value)
        right_hi[here, :] = high
        right_lo[here, :] = low
        high, low = split(value.T)
        left_hi[:, here] = high
        left_lo[:, here] = low

    high, low = split(proj[1024:ROWS, :])
    right_hi[1024:ROWS, :] = high
    right_lo[1024:ROWS, :] = low

    def half_gram(half, g):
        rows = pl.ds(pl.multiple_of(256 * half, 256), 256)
        there = slice(32 * g, 32 * g + 1024)
        total = dot(left_hi[rows, :], right_hi[there, :])
        total += dot(left_lo[rows, :], right_hi[there, :])
        total += dot(left_hi[rows, :], right_lo[there, :])
        return total

    def core_sum(g):
        return remote(gram_out.at[g], gram_in.at[g], cs_s.at[g], cs_r.at[g], device(x, y, z, 1 - core))

    for g in (0, 1):
        gram_out[g] = half_gram(1 - core, g)
        core_sum(g).start()
    for g in (0, 1):
        gram[g] = half_gram(core, g)
    for g in (0, 1):
        core_sum(g).wait_recv()
        gram[g] += gram_in[g]

    def to_plane(d):
        tx = around(x, lax.div(d, 4), 4)
        ty = around(y, lax.rem(d, 4), 4)
        src = gram.at[:, pl.ds(pl.multiple_of(64 * ty + 16 * tx, 16), 16), :]
        return remote(src, plane.at[x, y], pl_s.at[d - 1], pl_r.at[d - 1], device(tx, ty, z, core))

    @pl.loop(1, 16)
    def _(d):
        to_plane(d).start()

    plane[x, y] = gram[:, pl.ds(pl.multiple_of(64 * y + 16 * x, 16), 16), :]

    @pl.loop(1, 16)
    def _(d):
        to_plane(d).wait_recv()

    state = None
    for i in range(4):
        term = (plane[i, 0] + plane[i, 1]) + (plane[i, 2] + plane[i, 3])
        state = term if state is None else state + term
        states[i] = state

    def tile(t):
        return (t // 8, slice(8 * (t // 4 % 2), 8 * (t // 4 % 2) + 8), slice(128 * (t % 4), 128 * (t % 4) + 128))

    for t in range(NZ):
        tiles_out[t] = states[(3,) + tile(t)]

    def scatter(d):
        to = around(z, d, NZ)
        return remote(tiles_out.at[to], tiles_in.at[z], e1_s.at[d - 1], e1_r.at[d - 1], device(x, y, to, core))

    def bring_back(d):
        to = around(z, d, NZ)
        return remote(before_out.at[to], before_in.at[z], e2_s.at[d - 1], e2_r.at[d - 1], device(x, y, to, core))

    @pl.loop(1, NZ)
    def _(d):
        scatter(d).start()

    tiles_in[z] = tiles_out[z]

    @pl.loop(1, NZ)
    def _(d):
        scatter(d).wait_recv()

    running = jnp.zeros((8, 128), F32)
    for t in range(NZ):
        before_out[t] = running
        running = running + tiles_in[t]

    @pl.loop(1, NZ)
    def _(d):
        bring_back(d).start()

    before_in[z] = before_out[z]

    @pl.loop(1, NZ)
    def _(d):
        bring_back(d).wait_recv()

    own_rows = pl.ds(pl.multiple_of(16 * x, 16), 16)

    def to_owner(i):
        to = device(2 * (i // 2) + core, y, z, i % 2)
        return remote(final.at[i], out.at[0, :, own_rows, :], f_s.at[i], f_r.at[x], to)

    def mine(i):
        return jnp.logical_and(x == 2 * (i // 2) + core, core == i % 2)

    for i in range(4):
        count = ((4 * z + i + 1) * (LAG_DEV * P_SIZE)).astype(F32)
        for t in range(NZ):
            final[(i,) + tile(t)] = (before_in[t] + states[(i,) + tile(t)]) / count

        @pl.when(mine(i))
        def _():
            out[0, :, own_rows, :] = final[i]

        @pl.when(jnp.logical_not(mine(i)))
        def _():
            to_owner(i).start()

    def from_source(i):
        rows = pl.ds(16 * i, 16)
        here = out.at[0, :, rows, :]
        return remote(final.at[0], here, f_s.at[0], f_r.at[i], device(x, y, z, 1 - core))

    for i in range(4):
        @pl.when(jnp.logical_not(jnp.logical_and(x == i, core == x_lo)))
        def _():
            from_source(i).wait_recv()

    @pl.loop(1, NZ)
    def _(d):
        level1(d, z).wait_send()
        to_plane(d).wait_send()
        scatter(d).wait_send()
        bring_back(d).wait_send()

    @pl.when(swapped)
    def _():
        to_block().wait_send()

    @pl.when(lag > 0)
    def _():
        to_before().wait_send()

    for q in range(CHUNKS):
        for d in (1, 2, 3):
            level2(q, d).wait_send()

        def act(which):
            for d in (1, 2, 3):
                level3(q, d, which).wait_send()

        by_core(act)
        level4(q).wait_send()
    for g in (0, 1):
        core_sum(g).wait_send()
    for i in range(4):
        @pl.when(jnp.logical_not(mine(i)))
        def _():
            to_owner(i).wait_send()


def body(markov, basis):
    vmem = pl.BlockSpec(memory_space=pltpu.VMEM)
    counts = [2, 2, 15, 15, 12, 12, 12, 12, 4, 4, 2, 2, 15, 15, 15, 15, 15, 15, 4, 4]
    return pl.pallas_call(
        kernel,
        out_shape=jax.ShapeDtypeStruct((1, 2, 64, 512), F32),
        in_specs=[vmem, vmem],
        out_specs=vmem,
        scratch_shapes=[
            pltpu.VMEM((16, 32, 128), F32),
            pltpu.VMEM((2, 16, 32, 128), F32),
            pltpu.VMEM((2080, 768), BF16),
            pltpu.VMEM((16, 2, 2, 4, 8, 512), F32),
            pltpu.VMEM((768, 512), BF16),
            pltpu.VMEM((ROWS, 512), F32),
            pltpu.VMEM((ROWS, 512), BF16),
            pltpu.VMEM((ROWS, 512), BF16),
            pltpu.VMEM((512, 1024), BF16),
            pltpu.VMEM((512, 1024), BF16),
            pltpu.VMEM((2, 256, 512), F32),
            pltpu.VMEM((2, 256, 512), F32),
            pltpu.VMEM((2, 256, 512), F32),
            pltpu.VMEM((4, 4, 2, 16, 512), F32),
            pltpu.VMEM((4, 2, 16, 512), F32),
            pltpu.VMEM((NZ, 8, 128), F32),
            pltpu.VMEM((NZ, 8, 128), F32),
            pltpu.VMEM((NZ, 8, 128), F32),
            pltpu.VMEM((NZ, 8, 128), F32),
            pltpu.VMEM((4, 2, 16, 512), F32),
        ]
        + [pltpu.SemaphoreType.DMA((n,)) for n in counts],
        compiler_params=pltpu.CompilerParams(
            collective_id=0, has_side_effects=True, vmem_limit_bytes=48 * 1024 * 1024
        ),
        cost_estimate=pl.CostEstimate(flops=10_000_000_000, bytes_accessed=1_000_000, transcendentals=0),
    )(markov, basis)


def solution(mesh):
    placed = (P("lag", "out", None), P("lag", None))
    return jax.shard_map(
        body, mesh=mesh, in_specs=placed, out_specs=P("lag", None, "out", None), check_vma=False
    )
```

```python
import functools

import jax
import jax.numpy as jnp
from jax import lax
from jax.experimental import pallas as pl
from jax.experimental.pallas import tpu as pltpu
from jax.sharding import PartitionSpec as P

P_SIZE = 256
LAG_DEV = 32
MESH = pl.DeviceIdType.MESH
F32 = jnp.float32
BF16 = jnp.bfloat16

NZ = 16
CHUNKS = 8
SECOND, THIRD, LAST = 3, 6, 7
ROWS = 1056
TILE_M = 528


def split(value):
    high = value.astype(BF16)
    low = (value - high.astype(F32)).astype(BF16)
    return high, low


def device(x, y, z, core):
    return (4 * z + 2 * lax.div(x, 2) + core, 4 * lax.rem(x, 2) + y)


def dot(a, b):
    return jnp.dot(a, b, preferred_element_type=F32)


def kernel(
    markov_hbm, basis, out,
    markov, packed, pairs, lhs, gathered, weights, proj, right_hi, right_lo, left_hi, left_lo,
    gram_out, gram_in, gram, plane, states, tiles_out, tiles_in, before_out, before_in, final,
    mk_s, mk_r, b1_s, b1_r, b2_s, b2_r, b3_s, b3_r, b4_s, b4_r, cs_s, cs_r, pl_s, pl_r,
    e1_s, e1_r, e2_s, e2_r, f_s, f_r, in_s,
):
    lag = lax.axis_index("lag")
    chan = lax.axis_index("out")
    z = lax.div(lag, 4)
    x_hi = lax.rem(lax.div(lag, 2), 2)
    core = lax.rem(lag, 2)
    x_lo = lax.div(chan, 4)
    y = lax.rem(chan, 4)
    x = 2 * x_hi + x_lo
    block = 4 * z + x
    swapped = core != x_lo

    def remote(src, dst, send, recv, to):
        return pltpu.make_async_remote_copy(
            src_ref=src, dst_ref=dst, send_sem=send, recv_sem=recv, device_id=to, device_id_type=MESH
        )

    def around(value, step, size):
        return lax.rem(value + step, size)

    rows8 = pl.ds(pl.multiple_of(8 * y, 8), 8)
    cols = pl.ds(pl.multiple_of(256 * x_lo, 256), 256)
    take_markov = pltpu.make_async_copy(markov_hbm, markov, in_s.at[0])
    take_basis = pltpu.make_async_copy(
        basis.at[rows8, cols], gathered.at[z, x_hi, core, y, :, cols], in_s.at[1]
    )
    take_markov.start()
    take_basis.start()

    drains = []

    def loop_drain(make, count):
        def act():
            @pl.loop(1, count)
            def _(d):
                make(d).wait_send()

        drains.append(act)

    def when_drain(condition, make):
        def act():
            @pl.when(condition)
            def _():
                make().wait_send()

        drains.append(act)

    barrier = pltpu.get_barrier_semaphore()

    def greet(to):
        pl.semaphore_signal(barrier, inc=1, device_id=to, device_id_type=MESH)

    @pl.loop(1, NZ)
    def _(d):
        greet(device(x, y, around(z, d, NZ), core))

    @pl.loop(1, 16)
    def _(d):
        greet(device(around(x, lax.div(d, 4), 4), around(y, lax.rem(d, 4), 4), z, core))

    @pl.loop(0, 4)
    def _(d):
        greet(device(around(x, d, 4), y, z, 1 - core))

    gives_down = jnp.logical_and(lax.rem(lag, 4) == 0, z > 0)
    takes_up = jnp.logical_and(x == 3, z < NZ - 1)

    @pl.when(gives_down)
    def _():
        greet(device(3, y, z - 1, x_lo))

    @pl.when(takes_up)
    def _():
        greet((4 * (z + 1), 4 * core + y))

    take_markov.wait()
    for t in range(LAG_DEV // 2):
        packed[t] = jnp.concatenate([markov[2 * t], markov[2 * t + 1]], axis=-1)

    take_basis.wait()
    pl.semaphore_wait(barrier, 34 + gives_down.astype(jnp.int32) + takes_up.astype(jnp.int32))


    def level1(d, zz):
        piece = gathered.at[zz, x_hi, core, y, :, cols]
        return remote(piece, piece, b1_s.at[d - 1], b1_r.at[d - 1], device(x, y, around(z, d, NZ), core))

    @pl.loop(0, NZ - 1)
    def _(k):
        near = lax.div(k, 2)
        level1(jnp.where(lax.rem(k, 2) == 0, near + 1, NZ - 1 - near), z).start()

    loop_drain(lambda d: level1(d, z), NZ)

    def to_block():
        return remote(packed, pairs.at[0], mk_s.at[0], mk_r.at[0], device(2 * x_hi + core, y, z, x_lo))

    def to_before():
        earlier = lag - 1
        to = device(lax.rem(earlier, 4), y, lax.div(earlier, 4), x_lo)
        return remote(packed, pairs.at[1], mk_s.at[1], mk_r.at[1], to)

    @pl.when(swapped)
    def _():
        to_block().start()

    @pl.when(lag > 0)
    def _():
        to_before().start()

    when_drain(swapped, to_block)
    when_drain(lag > 0, to_before)

    @pl.when(jnp.logical_not(swapped))
    def _():
        pairs[0] = packed[...]

    @pl.when(block == 4 * NZ - 1)
    def _():
        pairs[1] = jnp.zeros_like(packed)

    def chunk_of(q):
        away = (q + 1) // 2 if q % 2 else CHUNKS - q // 2
        return lax.rem(lax.div(z, 2) + away, CHUNKS)

    def zs_of(q):
        return pl.ds(2 * chunk_of(q), 2)

    def wait_level1(q):
        @pl.loop(0, 2)
        def _(i):
            source = 2 * chunk_of(q) + i
            d = lax.rem(z - source + NZ, NZ)

            @pl.when(d > 0)
            def _():
                level1(d, source).wait_recv()

    def level2(q, d):
        piece = gathered.at[zs_of(q), x_hi, core, y, :, cols]
        x_next, y_next = device(around(x, d, 4), y, z, core), device(x, around(y, d, 4), z, core)
        to = tuple(jnp.where(core == 0, b, a) for a, b in zip(x_next, y_next))
        slot = 3 * q + d - 1
        return remote(piece, piece, b2_s.at[slot], b2_r.at[slot], to)

    def level3(q, d, x_last):
        slot = 3 * q + d - 1
        if x_last:
            piece = gathered.at[zs_of(q), x_hi, core, :, :, cols]
            to = device(around(x, d, 4), y, z, core)
        else:
            piece = gathered.at[zs_of(q), :, core, y]
            to = device(x, around(y, d, 4), z, core)
        return remote(piece, piece, b3_s.at[slot], b3_r.at[slot], to)

    def by_order(act):
        for x_last in (True, False):
            @pl.when((core == 0) == x_last)
            def _():
                act(x_last)

    def level4(q):
        piece = gathered.at[zs_of(q), :, core]
        return remote(piece, piece, b4_s.at[q], b4_r.at[q], device(x, y, z, 1 - core))

    def wait2_start3(q):
        for d in (1, 2, 3):
            level2(q, d).wait_recv()

        def act(x_last):
            for d in (1, 2, 3):
                level3(q, d, x_last).start()

        def drain(x_last):
            for d in (1, 2, 3):
                level3(q, d, x_last).wait_send()

        by_order(act)
        drains.append(lambda: by_order(drain))

    def wait3_start4(q):
        def act(x_last):
            for d in (1, 2, 3):
                level3(q, d, x_last).wait_recv()

        by_order(act)
        level4(q).start()
        drains.append(lambda: level4(q).wait_send())

    def wait1_start2(q):
        wait_level1(q)
        for d in (1, 2, 3):
            level2(q, d).start()

        def drain():
            for d in (1, 2, 3):
                level2(q, d).wait_send()

        drains.append(drain)

    def build_lhs():
        @pl.when(swapped)
        def _():
            to_block().wait_recv()

        @pl.when(block < 4 * NZ - 1)
        def _():
            to_before().wait_recv()

        first_half = lax.broadcasted_iota(jnp.int32, (32, 128), 1) < 64

        def put(t, value):
            high, low = split(value)
            for place, part in ((0, high), (256, low), (512, high)):
                lhs[pl.ds(pl.multiple_of(32 * t + 64, 32), 32), place : place + 128] = part
                lhs[pl.ds(pl.multiple_of(32 * t, 32), 32), place + 128 : place + 256] = part

        def both(t, this, following):
            put(2 * t, this)
            put(2 * t + 1, jnp.where(first_half, pltpu.roll(this, 64, 1), pltpu.roll(following, 64, 1)))

        for side in (0, 1):
            @pl.loop(0, 15)
            def _(t):
                both(16 * side + t, pairs[side, t], pairs[side, t + 1])

        both(15, pairs[0, 15], pairs[1, 0])
        put(62, pairs[1, 15])

    def compute(q):
        level4(q).wait_recv()

        part = chunk_of(q)
        for i in range(2):
            for h in range(2):
                for w in range(2):
                    high, low = split(gathered[2 * part + i, h, w].reshape(32, 512))
                    at = 128 * i + 64 * h + 32 * w
                    weights[at : at + 32, :] = high
                    weights[256 + at : 288 + at, :] = high
                    weights[512 + at : 544 + at, :] = low

        @pl.loop(0, ROWS // TILE_M)
        def _(m):
            here = pl.ds(pl.multiple_of(TILE_M * m, 16), TILE_M)
            there = pl.ds(pl.multiple_of(128 * part + 64 + TILE_M * m, 16), TILE_M)
            proj[here, :] += dot(lhs[there, :], weights[...])


    proj[...] = jnp.zeros_like(proj)
    for step in range(CHUNKS + LAST):
        if step < CHUNKS:
            wait1_start2(step)
        if 0 <= step - SECOND < CHUNKS:
            wait2_start3(step - SECOND)
        if 0 <= step - THIRD < CHUNKS:
            wait3_start4(step - THIRD)
        if step == LAST:
            build_lhs()
        if 0 <= step - LAST < CHUNKS:
            compute(step - LAST)


    @pl.loop(0, 8)
    def _(i):
        here = pl.ds(pl.multiple_of(128 * i, 128), 128)
        value = proj[here, :]
        high, low = split(value)
        right_hi[here, :] = high
        right_lo[here, :] = low
        high, low = split(value.T)
        left_hi[:, here] = high
        left_lo[:, here] = low

    high, low = split(proj[1024:ROWS, :])
    right_hi[1024:ROWS, :] = high
    right_lo[1024:ROWS, :] = low

    def half_gram(half, g):
        rows = pl.ds(pl.multiple_of(256 * half, 256), 256)
        there = slice(32 * g, 32 * g + 1024)
        total = dot(left_hi[rows, :], right_hi[there, :])
        total += dot(left_lo[rows, :], right_hi[there, :])
        total += dot(left_hi[rows, :], right_lo[there, :])
        return total


    def core_sum(g):
        return remote(gram_out.at[g], gram_in.at[g], cs_s.at[g], cs_r.at[g], device(x, y, z, 1 - core))

    def to_plane(g, d):
        tx = around(x, lax.div(d, 4), 4)
        ty = around(y, lax.rem(d, 4), 4)
        src = gram.at[g, pl.ds(pl.multiple_of(64 * ty + 16 * tx, 16), 16), :]
        slot = 15 * g + d - 1
        return remote(src, plane.at[g, x, y], pl_s.at[slot], pl_r.at[slot], device(tx, ty, z, core))

    def give_half(g):
        gram_out[g] = half_gram(1 - core, g)
        core_sum(g).start()
        drains.append(lambda: core_sum(g).wait_send())

    def give_plane(g):
        core_sum(g).wait_recv()
        gram[g] += gram_in[g]

        @pl.loop(1, 16)
        def _(d):
            to_plane(g, d).start()

        plane[g, x, y] = gram[g, pl.ds(pl.multiple_of(64 * y + 16 * x, 16), 16), :]
        loop_drain(functools.partial(to_plane, g), 16)

    give_half(0)
    gram[0] = half_gram(core, 0)
    give_half(1)
    give_plane(0)
    gram[1] = half_gram(core, 1)
    give_plane(1)

    def tile(t):
        return (slice(8 * (t // 4), 8 * (t // 4) + 8), slice(128 * (t % 4), 128 * (t % 4) + 128))

    def scatter(d):
        to = around(z, d, NZ)
        return remote(tiles_out.at[to], tiles_in.at[z], e1_s.at[d - 1], e1_r.at[d - 1], device(x, y, to, core))

    def bring_back(d):
        to = around(z, d, NZ)
        return remote(before_out.at[to], before_in.at[z], e2_s.at[d - 1], e2_r.at[d - 1], device(x, y, to, core))

    def owners(g, act):
        @pl.loop(0, NZ // 2)
        def _(t):
            d = lax.rem(2 * t + g - z + NZ, NZ)

            @pl.when(d > 0)
            def _():
                act(d)

    def give_tiles(g):
        @pl.loop(1, 16)
        def _(d):
            to_plane(g, d).wait_recv()

        state = None
        for i in range(4):
            term = (plane[g, i, 0] + plane[g, i, 1]) + (plane[g, i, 2] + plane[g, i, 3])
            state = term if state is None else state + term
            states[i, g] = state
        for t in range(NZ // 2):
            tiles_out[2 * t + g] = states[(3, g) + tile(t)]
        owners(g, lambda d: scatter(d).start())

    def give_before(g):
        @pl.when(lax.rem(z, 2) == g)
        def _():
            tiles_in[z] = tiles_out[z]

            @pl.loop(1, NZ)
            def _(d):
                scatter(d).wait_recv()

            running = jnp.zeros((8, 128), F32)
            for t in range(NZ):
                before_out[t] = running
                running = running + tiles_in[t]

            @pl.loop(1, NZ)
            def _(d):
                bring_back(d).start()

            before_in[z] = before_out[z]

    own_rows = pl.ds(pl.multiple_of(16 * x, 16), 16)

    def to_owner(i, g):
        to = device(2 * (i // 2) + core, y, z, i % 2)
        here = out.at[0, g, own_rows, :]
        return remote(final.at[i, g], here, f_s.at[4 * g + i], f_r.at[4 * g + x], to)

    def mine(i):
        return jnp.logical_and(x == 2 * (i // 2) + core, core == i % 2)

    def give_means(g):
        def arrived(d):
            bring_back(NZ - d).wait_recv()

        owners(g, arrived)
        for i in range(4):
            count = ((4 * z + i + 1) * (LAG_DEV * P_SIZE)).astype(F32)
            for t in range(NZ // 2):
                final[(i, g) + tile(t)] = (before_in[2 * t + g] + states[(i, g) + tile(t)]) / count

            @pl.when(mine(i))
            def _():
                out[0, g, own_rows, :] = final[i, g]

            @pl.when(jnp.logical_not(mine(i)))
            def _():
                to_owner(i, g).start()

            when_drain(jnp.logical_not(mine(i)), functools.partial(to_owner, i, g))

    def take_means(g):
        for i in range(4):
            @pl.when(jnp.logical_not(jnp.logical_and(x == i, core == x_lo)))
            def _():
                here = out.at[0, g, pl.ds(16 * i, 16), :]
                at = 4 * g + i
                remote(final.at[0, g], here, f_s.at[at], f_r.at[at], device(x, y, z, 1 - core)).wait_recv()

    for act in (give_tiles, give_before, give_means, take_means):
        for g in (0, 1):
            act(g)

    def sent_along_z():
        @pl.loop(1, NZ)
        def _(d):
            scatter(d).wait_send()

    def sent_back():
        @pl.loop(1, NZ)
        def _(d):
            bring_back(d).wait_send()

    drains += [sent_along_z, sent_back]

    for act in drains:
        act()


def body(markov, basis):
    vmem = pl.BlockSpec(memory_space=pltpu.VMEM)
    hbm = pl.BlockSpec(memory_space=pltpu.HBM)
    counts = [2, 2, 15, 15, 24, 24, 24, 24, 8, 8, 2, 2, 30, 30, 15, 15, 15, 15, 8, 8, 2]
    return pl.pallas_call(
        kernel,
        out_shape=jax.ShapeDtypeStruct((1, 2, 64, 512), F32),
        in_specs=[hbm, hbm],
        out_specs=vmem,
        scratch_shapes=[
            pltpu.VMEM((32, 32, 64), F32),
            pltpu.VMEM((16, 32, 128), F32),
            pltpu.VMEM((2, 16, 32, 128), F32),
            pltpu.VMEM((2080, 768), BF16),
            pltpu.VMEM((16, 2, 2, 4, 8, 512), F32),
            pltpu.VMEM((768, 512), BF16),
            pltpu.VMEM((ROWS, 512), F32),
            pltpu.VMEM((ROWS, 512), BF16),
            pltpu.VMEM((ROWS, 512), BF16),
            pltpu.VMEM((512, 1024), BF16),
            pltpu.VMEM((512, 1024), BF16),
            pltpu.VMEM((2, 256, 512), F32),
            pltpu.VMEM((2, 256, 512), F32),
            pltpu.VMEM((2, 256, 512), F32),
            pltpu.VMEM((2, 4, 4, 16, 512), F32),
            pltpu.VMEM((4, 2, 16, 512), F32),
            pltpu.VMEM((NZ, 8, 128), F32),
            pltpu.VMEM((NZ, 8, 128), F32),
            pltpu.VMEM((NZ, 8, 128), F32),
            pltpu.VMEM((NZ, 8, 128), F32),
            pltpu.VMEM((4, 2, 16, 512), F32),
        ]
        + [pltpu.SemaphoreType.DMA((n,)) for n in counts],
        compiler_params=pltpu.CompilerParams(
            collective_id=0, has_side_effects=True, vmem_limit_bytes=62 * 1024 * 1024
        ),
        cost_estimate=pl.CostEstimate(flops=10_000_000_000, bytes_accessed=1_000_000, transcendentals=0),
    )(markov, basis)


def solution(mesh):
    placed = (P("lag", "out", None), P("lag", None))
    return jax.shard_map(
        body, mesh=mesh, in_specs=placed, out_specs=P("lag", None, "out", None), check_vma=False
    )
```

```python
import functools

import jax
import jax.numpy as jnp
from jax import lax
from jax.experimental import pallas as pl
from jax.experimental.pallas import tpu as pltpu
from jax.sharding import PartitionSpec as P

P_SIZE = 256
LAG_DEV = 32
MESH = pl.DeviceIdType.MESH
F32 = jnp.float32
BF16 = jnp.bfloat16

NZ = 16
CHUNKS = 8
X_LAST = (0, 1, 2, 3, 4, 5, 6, 7)
ORDER = (
    "M0", "A0", "M1", "A1", "M2", "A2", "M3", "B0", "A3", "A4", "B1", "B2", "A5", "A6", "B3", "B4", "L0", "A7", "B5", "B6",
    "C0", "C1", "D0", "C2", "D1", "B7", "C3", "D2", "C4", "D3", "C5", "D4", "C6", "D5", "C7", "D6", "D7",
)
ROWS = 1056
TILE_M = 528


def split(value):
    high = value.astype(BF16)
    low = (value - high.astype(F32)).astype(BF16)
    return high, low


def device(x, y, z, core):
    return (4 * z + 2 * lax.div(x, 2) + core, 4 * lax.rem(x, 2) + y)


def dot(a, b):
    return jnp.dot(a, b, preferred_element_type=F32)


def kernel(
    markov_hbm, basis, out,
    markov, packed, pairs, lhs, gathered, weights, proj, right_hi, right_lo, left_hi, left_lo,
    gram_out, gram_in, gram, plane, states, tiles_out, tiles_in, before_out, before_in, final,
    mk_s, mk_r, b1_s, b1_r, b2_s, b2_r, b3_s, b3_r, b4_s, b4_r, cs_s, cs_r, pl_s, pl_r,
    e1_s, e1_r, e2_s, e2_r, f_s, f_r, in_s,
):
    lag = lax.axis_index("lag")
    chan = lax.axis_index("out")
    z = lax.div(lag, 4)
    x_hi = lax.rem(lax.div(lag, 2), 2)
    core = lax.rem(lag, 2)
    x_lo = lax.div(chan, 4)
    y = lax.rem(chan, 4)
    x = 2 * x_hi + x_lo
    block = 4 * z + x
    swapped = core != x_lo

    def remote(src, dst, send, recv, to):
        return pltpu.make_async_remote_copy(
            src_ref=src, dst_ref=dst, send_sem=send, recv_sem=recv, device_id=to, device_id_type=MESH
        )

    def around(value, step, size):
        return lax.rem(value + step, size)

    rows8 = pl.ds(pl.multiple_of(8 * y, 8), 8)
    cols = pl.ds(pl.multiple_of(256 * x_lo, 256), 256)
    take_markov = pltpu.make_async_copy(markov_hbm, markov, in_s.at[0])
    take_basis = pltpu.make_async_copy(
        basis.at[rows8, cols], gathered.at[z, x_hi, core, y, :, cols], in_s.at[1]
    )
    take_markov.start()
    take_basis.start()

    drains = []

    def loop_drain(make, count):
        def act():
            @pl.loop(1, count)
            def _(d):
                make(d).wait_send()

        drains.append(act)

    def when_drain(condition, make):
        def act():
            @pl.when(condition)
            def _():
                make().wait_send()

        drains.append(act)

    barrier = pltpu.get_barrier_semaphore()

    def greet(to):
        pl.semaphore_signal(barrier, inc=1, device_id=to, device_id_type=MESH)

    @pl.loop(1, NZ)
    def _(d):
        greet(device(x, y, around(z, d, NZ), core))

    @pl.loop(1, 16)
    def _(d):
        greet(device(around(x, lax.div(d, 4), 4), around(y, lax.rem(d, 4), 4), z, core))

    @pl.loop(0, 4)
    def _(d):
        greet(device(around(x, d, 4), y, z, 1 - core))

    gives_down = jnp.logical_and(lax.rem(lag, 4) == 0, z > 0)
    takes_up = jnp.logical_and(x == 3, z < NZ - 1)

    @pl.when(gives_down)
    def _():
        greet(device(3, y, z - 1, x_lo))

    @pl.when(takes_up)
    def _():
        greet((4 * (z + 1), 4 * core + y))

    take_markov.wait()
    for t in range(LAG_DEV // 2):
        packed[t] = jnp.concatenate([markov[2 * t], markov[2 * t + 1]], axis=-1)

    take_basis.wait()
    pl.semaphore_wait(barrier, 34 + gives_down.astype(jnp.int32) + takes_up.astype(jnp.int32))


    def level1(d, zz):
        piece = gathered.at[zz, x_hi, core, y, :, cols]
        return remote(piece, piece, b1_s.at[d - 1], b1_r.at[d - 1], device(x, y, around(z, d, NZ), core))

    @pl.loop(0, NZ - 1)
    def _(k):
        near = lax.div(k, 2)
        level1(jnp.where(lax.rem(k, 2) == 0, near + 1, NZ - 1 - near), z).start()

    loop_drain(lambda d: level1(d, z), NZ)

    def to_block(i):
        part = pl.ds(4 * i, 4)
        to = device(2 * x_hi + core, y, z, x_lo)
        return remote(packed.at[part], pairs.at[0, part], mk_s.at[0, i], mk_r.at[0, i], to)

    def to_before(i):
        part = pl.ds(4 * i, 4)
        earlier = lag - 1
        to = device(lax.rem(earlier, 4), y, lax.div(earlier, 4), x_lo)
        return remote(packed.at[part], pairs.at[1, part], mk_s.at[1, i], mk_r.at[1, i], to)

    def give_quarter(i):
        @pl.when(swapped)
        def _():
            to_block(i).start()

        @pl.when(lag > 0)
        def _():
            to_before(i).start()

        when_drain(swapped, functools.partial(to_block, i))
        when_drain(lag > 0, functools.partial(to_before, i))

    @pl.when(jnp.logical_not(swapped))
    def _():
        pairs[0] = packed[...]

    @pl.when(block == 4 * NZ - 1)
    def _():
        pairs[1] = jnp.zeros_like(packed)

    def chunk_of(q):
        away = (q + 1) // 2 if q % 2 else CHUNKS - q // 2
        return lax.rem(lax.div(z, 2) + away, CHUNKS)

    def zs_of(q):
        return pl.ds(2 * chunk_of(q), 2)

    def wait_level1(q):
        @pl.loop(0, 2)
        def _(i):
            source = 2 * chunk_of(q) + i
            d = lax.rem(z - source + NZ, NZ)

            @pl.when(d > 0)
            def _():
                level1(d, source).wait_recv()

    def level2(q, d):
        piece = gathered.at[zs_of(q), x_hi, core, y, :, cols]
        x_next, y_next = device(around(x, d, 4), y, z, core), device(x, around(y, d, 4), z, core)
        if q in X_LAST:
            to = tuple(jnp.where(core == 0, b, a) for a, b in zip(x_next, y_next))
        else:
            to = x_next
        slot = 3 * q + d - 1
        return remote(piece, piece, b2_s.at[slot], b2_r.at[slot], to)

    def level3(q, d, x_last):
        slot = 3 * q + d - 1
        if x_last:
            piece = gathered.at[zs_of(q), x_hi, core, :, :, cols]
            to = device(around(x, d, 4), y, z, core)
        else:
            piece = gathered.at[zs_of(q), :, core, y]
            to = device(x, around(y, d, 4), z, core)
        return remote(piece, piece, b3_s.at[slot], b3_r.at[slot], to)

    def by_order(q, act):
        if q not in X_LAST:
            act(False)
            return

        for x_last in (True, False):
            @pl.when((core == 0) == x_last)
            def _():
                act(x_last)

    def level4(q):
        piece = gathered.at[zs_of(q), :, core]
        return remote(piece, piece, b4_s.at[q], b4_r.at[q], device(x, y, z, 1 - core))

    def wait2_start3(q):
        for d in (1, 2, 3):
            level2(q, d).wait_recv()

        def act(x_last):
            for d in (1, 2, 3):
                level3(q, d, x_last).start()

        def drain(x_last):
            for d in (1, 2, 3):
                level3(q, d, x_last).wait_send()

        by_order(q, act)
        drains.append(lambda: by_order(q, drain))

    def wait3_start4(q):
        def act(x_last):
            for d in (1, 2, 3):
                level3(q, d, x_last).wait_recv()

        by_order(q, act)
        level4(q).start()
        drains.append(lambda: level4(q).wait_send())

    def wait1_start2(q):
        wait_level1(q)
        for d in (1, 2, 3):
            level2(q, d).start()

        def drain():
            for d in (1, 2, 3):
                level2(q, d).wait_send()

        drains.append(drain)

    def build_lhs(_):
        proj[...] = jnp.zeros_like(proj)

        @pl.when(swapped)
        def _():
            for i in range(4):
                to_block(i).wait_recv()

        @pl.when(block < 4 * NZ - 1)
        def _():
            for i in range(4):
                to_before(i).wait_recv()

        first_half = lax.broadcasted_iota(jnp.int32, (32, 128), 1) < 64

        def put(t, value):
            high, low = split(value)
            for place, part in ((0, high), (256, low), (512, high)):
                lhs[pl.ds(pl.multiple_of(32 * t + 64, 32), 32), place : place + 128] = part
                lhs[pl.ds(pl.multiple_of(32 * t, 32), 32), place + 128 : place + 256] = part

        def both(t, this, following):
            put(2 * t, this)
            put(2 * t + 1, jnp.where(first_half, pltpu.roll(this, 64, 1), pltpu.roll(following, 64, 1)))

        for side in (0, 1):
            @pl.loop(0, 15)
            def _(t):
                both(16 * side + t, pairs[side, t], pairs[side, t + 1])

        both(15, pairs[0, 15], pairs[1, 0])
        put(62, pairs[1, 15])

    def compute(q):
        level4(q).wait_recv()

        part = chunk_of(q)
        for i in range(2):
            for h in range(2):
                for w in range(2):
                    high, low = split(gathered[2 * part + i, h, w].reshape(32, 512))
                    at = 128 * i + 64 * h + 32 * w
                    weights[at : at + 32, :] = high
                    weights[256 + at : 288 + at, :] = high
                    weights[512 + at : 544 + at, :] = low

        @pl.loop(0, ROWS // TILE_M)
        def _(m):
            here = pl.ds(pl.multiple_of(TILE_M * m, 16), TILE_M)
            there = pl.ds(pl.multiple_of(128 * part + 64 + TILE_M * m, 16), TILE_M)
            proj[here, :] += dot(lhs[there, :], weights[...])


    acts = dict(M=give_quarter, L=build_lhs, A=wait1_start2, B=wait2_start3, C=wait3_start4, D=compute)
    for name in ORDER:
        acts[name[0]](int(name[1]))


    @pl.loop(0, 8)
    def _(i):
        here = pl.ds(pl.multiple_of(128 * i, 128), 128)
        value = proj[here, :]
        high, low = split(value)
        right_hi[here, :] = high
        right_lo[here, :] = low
        high, low = split(value.T)
        left_hi[:, here] = high
        left_lo[:, here] = low

    high, low = split(proj[1024:ROWS, :])
    right_hi[1024:ROWS, :] = high
    right_lo[1024:ROWS, :] = low

    def half_gram(half, g):
        rows = pl.ds(pl.multiple_of(256 * half, 256), 256)
        there = slice(32 * g, 32 * g + 1024)
        total = dot(left_hi[rows, :], right_hi[there, :])
        total += dot(left_lo[rows, :], right_hi[there, :])
        total += dot(left_hi[rows, :], right_lo[there, :])
        return total


    def core_sum(g):
        return remote(gram_out.at[g], gram_in.at[g], cs_s.at[g], cs_r.at[g], device(x, y, z, 1 - core))

    def to_plane(g, d):
        tx = around(x, lax.div(d, 4), 4)
        ty = around(y, lax.rem(d, 4), 4)
        src = gram.at[g, pl.ds(pl.multiple_of(64 * ty + 16 * tx, 16), 16), :]
        slot = 15 * g + d - 1
        return remote(src, plane.at[g, x, y], pl_s.at[slot], pl_r.at[slot], device(tx, ty, z, core))

    def give_half(g):
        gram_out[g] = half_gram(1 - core, g)
        core_sum(g).start()
        drains.append(lambda: core_sum(g).wait_send())

    def give_plane(g):
        core_sum(g).wait_recv()
        gram[g] += gram_in[g]

        @pl.loop(1, 16)
        def _(d):
            to_plane(g, d).start()

        plane[g, x, y] = gram[g, pl.ds(pl.multiple_of(64 * y + 16 * x, 16), 16), :]
        loop_drain(functools.partial(to_plane, g), 16)

    give_half(0)
    gram[0] = half_gram(core, 0)
    give_half(1)
    give_plane(0)
    gram[1] = half_gram(core, 1)
    give_plane(1)

    def tile(t):
        return (slice(8 * (t // 4), 8 * (t // 4) + 8), slice(128 * (t % 4), 128 * (t % 4) + 128))

    def scatter(d):
        to = around(z, d, NZ)
        return remote(tiles_out.at[to], tiles_in.at[z], e1_s.at[d - 1], e1_r.at[d - 1], device(x, y, to, core))

    def bring_back(d):
        to = around(z, d, NZ)
        return remote(before_out.at[to], before_in.at[z], e2_s.at[d - 1], e2_r.at[d - 1], device(x, y, to, core))

    def apart(k):
        half = lax.div(k + 1, 2)
        return jnp.where(lax.rem(k, 2) == 1, half, -half)

    def owners(g, act):
        @pl.loop(0, NZ // 2)
        def _(k):
            d = lax.rem(NZ // 2 - lax.rem(g + z, 2) + 2 * apart(k), NZ)

            @pl.when(d > 0)
            def _():
                act(d)

    def give_tiles(g):
        @pl.loop(1, 16)
        def _(d):
            to_plane(g, d).wait_recv()

        state = None
        for i in range(4):
            term = (plane[g, i, 0] + plane[g, i, 1]) + (plane[g, i, 2] + plane[g, i, 3])
            state = term if state is None else state + term
            states[i, g] = state
        for t in range(NZ // 2):
            tiles_out[2 * t + g] = states[(3, g) + tile(t)]
        owners(g, lambda d: scatter(d).start())

    def give_before(g):
        @pl.when(lax.rem(z, 2) == g)
        def _():
            tiles_in[z] = tiles_out[z]

            @pl.loop(1, NZ)
            def _(d):
                scatter(d).wait_recv()

            running = jnp.zeros((8, 128), F32)
            for t in range(NZ):
                before_out[t] = running
                running = running + tiles_in[t]

            @pl.loop(0, NZ - 1)
            def _(k):
                bring_back(NZ // 2 + apart(k)).start()

            before_in[z] = before_out[z]

    own_rows = pl.ds(pl.multiple_of(16 * x, 16), 16)

    def to_owner(i, g):
        to = device(2 * lax.div(i, 2) + core, y, z, lax.rem(i, 2))
        here = out.at[0, g, own_rows, :]
        return remote(final.at[i, g], here, f_s.at[4 * g + i], f_r.at[4 * g + x], to)

    def mine(i):
        return jnp.logical_and(x == 2 * lax.div(i, 2) + core, core == lax.rem(i, 2))

    def give_means(g):
        def arrived(d):
            bring_back(NZ - d).wait_recv()

        owners(g, arrived)
        for k in range(4):
            i = lax.rem(2 * (1 - x_hi) + k, 4)
            count = ((4 * z + i + 1) * (LAG_DEV * P_SIZE)).astype(F32)
            for t in range(NZ // 2):
                final[(i, g) + tile(t)] = (before_in[2 * t + g] + states[(i, g) + tile(t)]) / count

            @pl.when(mine(i))
            def _():
                out[0, g, own_rows, :] = final[i, g]

            @pl.when(jnp.logical_not(mine(i)))
            def _():
                to_owner(i, g).start()

            when_drain(jnp.logical_not(mine(i)), functools.partial(to_owner, i, g))

    def take_means(g):
        for i in range(4):
            @pl.when(jnp.logical_not(jnp.logical_and(x == i, core == x_lo)))
            def _():
                here = out.at[0, g, pl.ds(16 * i, 16), :]
                at = 4 * g + i
                remote(final.at[0, g], here, f_s.at[at], f_r.at[at], device(x, y, z, 1 - core)).wait_recv()

    for act in (give_tiles, give_before, give_means, take_means):
        for g in (0, 1):
            act(g)

    def sent_along_z():
        @pl.loop(1, NZ)
        def _(d):
            scatter(d).wait_send()

    def sent_back():
        @pl.loop(1, NZ)
        def _(d):
            bring_back(d).wait_send()

    drains += [sent_along_z, sent_back]

    for act in drains:
        act()


def body(markov, basis):
    vmem = pl.BlockSpec(memory_space=pltpu.VMEM)
    hbm = pl.BlockSpec(memory_space=pltpu.HBM)
    counts = [15, 15, 24, 24, 24, 24, 8, 8, 2, 2, 30, 30, 15, 15, 15, 15, 8, 8, 2]
    return pl.pallas_call(
        kernel,
        out_shape=jax.ShapeDtypeStruct((1, 2, 64, 512), F32),
        in_specs=[hbm, hbm],
        out_specs=vmem,
        scratch_shapes=[
            pltpu.VMEM((32, 32, 64), F32),
            pltpu.VMEM((16, 32, 128), F32),
            pltpu.VMEM((2, 16, 32, 128), F32),
            pltpu.VMEM((2080, 768), BF16),
            pltpu.VMEM((16, 2, 2, 4, 8, 512), F32),
            pltpu.VMEM((768, 512), BF16),
            pltpu.VMEM((ROWS, 512), F32),
            pltpu.VMEM((ROWS, 512), BF16),
            pltpu.VMEM((ROWS, 512), BF16),
            pltpu.VMEM((512, 1024), BF16),
            pltpu.VMEM((512, 1024), BF16),
            pltpu.VMEM((2, 256, 512), F32),
            pltpu.VMEM((2, 256, 512), F32),
            pltpu.VMEM((2, 256, 512), F32),
            pltpu.VMEM((2, 4, 4, 16, 512), F32),
            pltpu.VMEM((4, 2, 16, 512), F32),
            pltpu.VMEM((NZ, 8, 128), F32),
            pltpu.VMEM((NZ, 8, 128), F32),
            pltpu.VMEM((NZ, 8, 128), F32),
            pltpu.VMEM((NZ, 8, 128), F32),
            pltpu.VMEM((4, 2, 16, 512), F32),
        ]
        + [pltpu.SemaphoreType.DMA((2, 4))] * 2
        + [pltpu.SemaphoreType.DMA((n,)) for n in counts],
        compiler_params=pltpu.CompilerParams(
            collective_id=0, has_side_effects=True, vmem_limit_bytes=62 * 1024 * 1024
        ),
        cost_estimate=pl.CostEstimate(flops=10_000_000_000, bytes_accessed=1_000_000, transcendentals=0),
    )(markov, basis)


def solution(mesh):
    placed = (P("lag", "out", None), P("lag", None))
    return jax.shard_map(
        body, mesh=mesh, in_specs=placed, out_specs=P("lag", None, "out", None), check_vma=False
    )
```

```python
import functools

import jax
import jax.numpy as jnp
from jax import lax
from jax.experimental import pallas as pl
from jax.experimental.pallas import tpu as pltpu
from jax.sharding import PartitionSpec as P

P_SIZE = 256
LAG_DEV = 32
MESH = pl.DeviceIdType.MESH
F32 = jnp.float32
BF16 = jnp.bfloat16

NZ = 16
CHUNKS = 8
X_LAST = (0, 1, 2, 3, 4, 5, 6, 7)
ORDER = (
    "M0", "M1", "A0", "M2", "A1", "M3", "A2", "A3", "B0", "A4", "B1", "B2", "A5", "A6", "B3", "B4", "L0", "A7", "B5", "C0",
    "B6", "C1", "D0", "C2", "D1", "C3", "B7", "D2", "C4", "D3", "C5", "D4", "C6", "D5", "C7", "D6", "D7",
)
ROWS = 1056
TILE_M = 528


def split(value):
    high = value.astype(BF16)
    low = (value - high.astype(F32)).astype(BF16)
    return high, low


def device(x, y, z, core):
    return (4 * z + 2 * lax.div(x, 2) + core, 4 * lax.rem(x, 2) + y)


def dot(a, b):
    return jnp.dot(a, b, preferred_element_type=F32)


def kernel(
    markov_hbm, basis, out,
    markov, packed, pairs, lhs, gathered, weights, proj, right_hi, right_lo, left_hi, left_lo,
    gram_out, gram_in, gram, via, plane, states, tiles_out, tiles_in, before_out, before_in, final,
    mk_s, mk_r, b1_s, b1_r, b2_s, b2_r, b3_s, b3_r, b4_s, b4_r, cs_s, cs_r, via_s, via_r, pl_s, pl_r,
    e1_s, e1_r, e2_s, e2_r, f_s, f_r, in_s,
):
    lag = lax.axis_index("lag")
    chan = lax.axis_index("out")
    z = lax.div(lag, 4)
    x_hi = lax.rem(lax.div(lag, 2), 2)
    core = lax.rem(lag, 2)
    x_lo = lax.div(chan, 4)
    y = lax.rem(chan, 4)
    x = 2 * x_hi + x_lo
    block = 4 * z + x
    swapped = core != x_lo

    def remote(src, dst, send, recv, to):
        return pltpu.make_async_remote_copy(
            src_ref=src, dst_ref=dst, send_sem=send, recv_sem=recv, device_id=to, device_id_type=MESH
        )

    def around(value, step, size):
        return lax.rem(value + step, size)

    rows8 = pl.ds(pl.multiple_of(8 * y, 8), 8)
    cols = pl.ds(pl.multiple_of(256 * x_lo, 256), 256)
    take_markov = pltpu.make_async_copy(markov_hbm, markov, in_s.at[0])
    take_basis = pltpu.make_async_copy(
        basis.at[rows8, cols], gathered.at[z, x_hi, core, y, :, cols], in_s.at[1]
    )
    take_markov.start()
    take_basis.start()

    drains = []

    def loop_drain(make, count):
        def act():
            @pl.loop(1, count)
            def _(d):
                make(d).wait_send()

        drains.append(act)

    def when_drain(condition, make):
        def act():
            @pl.when(condition)
            def _():
                make().wait_send()

        drains.append(act)

    barrier = pltpu.get_barrier_semaphore()

    def greet(to):
        pl.semaphore_signal(barrier, inc=1, device_id=to, device_id_type=MESH)

    @pl.loop(1, NZ)
    def _(d):
        greet(device(x, y, around(z, d, NZ), core))

    @pl.loop(1, 16)
    def _(d):
        greet(device(around(x, lax.div(d, 4), 4), around(y, lax.rem(d, 4), 4), z, core))

    @pl.loop(0, 4)
    def _(d):
        greet(device(around(x, d, 4), y, z, 1 - core))

    gives_down = jnp.logical_and(lax.rem(lag, 4) == 0, z > 0)
    takes_up = jnp.logical_and(x == 3, z < NZ - 1)

    @pl.when(gives_down)
    def _():
        greet(device(3, y, z - 1, x_lo))

    @pl.when(takes_up)
    def _():
        greet((4 * (z + 1), 4 * core + y))

    take_markov.wait()
    for t in range(LAG_DEV // 2):
        packed[t] = jnp.concatenate([markov[2 * t], markov[2 * t + 1]], axis=-1)

    take_basis.wait()
    pl.semaphore_wait(barrier, 34 + gives_down.astype(jnp.int32) + takes_up.astype(jnp.int32))


    def level1(d, zz):
        piece = gathered.at[zz, x_hi, core, y, :, cols]
        return remote(piece, piece, b1_s.at[d - 1], b1_r.at[d - 1], device(x, y, around(z, d, NZ), core))

    @pl.loop(0, NZ - 1)
    def _(k):
        near = lax.div(k, 2)
        level1(jnp.where(lax.rem(k, 2) == 0, near + 1, NZ - 1 - near), z).start()

    loop_drain(lambda d: level1(d, z), NZ)

    def to_block(i):
        part = pl.ds(4 * i, 4)
        to = device(2 * x_hi + core, y, z, x_lo)
        return remote(packed.at[part], pairs.at[0, part], mk_s.at[0, i], mk_r.at[0, i], to)

    def to_before(i):
        part = pl.ds(4 * i, 4)
        earlier = lag - 1
        to = device(lax.rem(earlier, 4), y, lax.div(earlier, 4), x_lo)
        return remote(packed.at[part], pairs.at[1, part], mk_s.at[1, i], mk_r.at[1, i], to)

    def give_quarter(i):
        @pl.when(swapped)
        def _():
            to_block(i).start()

        @pl.when(lag > 0)
        def _():
            to_before(i).start()

        when_drain(swapped, functools.partial(to_block, i))
        when_drain(lag > 0, functools.partial(to_before, i))

    @pl.when(jnp.logical_not(swapped))
    def _():
        pairs[0] = packed[...]

    @pl.when(block == 4 * NZ - 1)
    def _():
        pairs[1] = jnp.zeros_like(packed)

    def chunk_of(q):
        away = (q + 1) // 2 if q % 2 else CHUNKS - q // 2
        return lax.rem(lax.div(z, 2) + away, CHUNKS)

    def zs_of(q):
        return pl.ds(2 * chunk_of(q), 2)

    def wait_level1(q):
        @pl.loop(0, 2)
        def _(i):
            source = 2 * chunk_of(q) + i
            d = lax.rem(z - source + NZ, NZ)

            @pl.when(d > 0)
            def _():
                level1(d, source).wait_recv()

    def level2(q, d):
        piece = gathered.at[zs_of(q), x_hi, core, y, :, cols]
        x_next, y_next = device(around(x, d, 4), y, z, core), device(x, around(y, d, 4), z, core)
        if q in X_LAST:
            to = tuple(jnp.where(core == 0, b, a) for a, b in zip(x_next, y_next))
        else:
            to = x_next
        slot = 3 * q + d - 1
        return remote(piece, piece, b2_s.at[slot], b2_r.at[slot], to)

    def level3(q, d, x_last):
        slot = 3 * q + d - 1
        if x_last:
            piece = gathered.at[zs_of(q), x_hi, core, :, :, cols]
            to = device(around(x, d, 4), y, z, core)
        else:
            piece = gathered.at[zs_of(q), :, core, y]
            to = device(x, around(y, d, 4), z, core)
        return remote(piece, piece, b3_s.at[slot], b3_r.at[slot], to)

    def by_order(q, act):
        if q not in X_LAST:
            act(False)
            return

        for x_last in (True, False):
            @pl.when((core == 0) == x_last)
            def _():
                act(x_last)

    def level4(q):
        piece = gathered.at[zs_of(q), :, core]
        return remote(piece, piece, b4_s.at[q], b4_r.at[q], device(x, y, z, 1 - core))

    def wait2_start3(q):
        for d in (1, 2, 3):
            level2(q, d).wait_recv()

        def act(x_last):
            for d in (1, 2, 3):
                level3(q, d, x_last).start()

        def drain(x_last):
            for d in (1, 2, 3):
                level3(q, d, x_last).wait_send()

        by_order(q, act)
        drains.append(lambda: by_order(q, drain))

    def wait3_start4(q):
        def act(x_last):
            for d in (1, 2, 3):
                level3(q, d, x_last).wait_recv()

        by_order(q, act)
        level4(q).start()
        drains.append(lambda: level4(q).wait_send())

    def wait1_start2(q):
        wait_level1(q)
        for d in (1, 2, 3):
            level2(q, d).start()

        def drain():
            for d in (1, 2, 3):
                level2(q, d).wait_send()

        drains.append(drain)

    def build_lhs(_):
        proj[...] = jnp.zeros_like(proj)

        @pl.when(swapped)
        def _():
            for i in range(4):
                to_block(i).wait_recv()

        @pl.when(block < 4 * NZ - 1)
        def _():
            for i in range(4):
                to_before(i).wait_recv()

        first_half = lax.broadcasted_iota(jnp.int32, (32, 128), 1) < 64

        def put(t, value):
            high, low = split(value)
            for place, part in ((0, high), (256, low), (512, high)):
                lhs[pl.ds(pl.multiple_of(32 * t + 64, 32), 32), place : place + 128] = part
                lhs[pl.ds(pl.multiple_of(32 * t, 32), 32), place + 128 : place + 256] = part

        def both(t, this, following):
            put(2 * t, this)
            put(2 * t + 1, jnp.where(first_half, pltpu.roll(this, 64, 1), pltpu.roll(following, 64, 1)))

        for side in (0, 1):
            @pl.loop(0, 15)
            def _(t):
                both(16 * side + t, pairs[side, t], pairs[side, t + 1])

        both(15, pairs[0, 15], pairs[1, 0])
        put(62, pairs[1, 15])

    def compute(q):
        level4(q).wait_recv()

        part = chunk_of(q)
        for i in range(2):
            for h in range(2):
                for w in range(2):
                    high, low = split(gathered[2 * part + i, h, w].reshape(32, 512))
                    at = 128 * i + 64 * h + 32 * w
                    weights[at : at + 32, :] = high
                    weights[256 + at : 288 + at, :] = high
                    weights[512 + at : 544 + at, :] = low

        @pl.loop(0, ROWS // TILE_M)
        def _(m):
            here = pl.ds(pl.multiple_of(TILE_M * m, 16), TILE_M)
            there = pl.ds(pl.multiple_of(128 * part + 64 + TILE_M * m, 16), TILE_M)
            proj[here, :] += dot(lhs[there, :], weights[...])


    acts = dict(M=give_quarter, L=build_lhs, A=wait1_start2, B=wait2_start3, C=wait3_start4, D=compute)
    for name in ORDER:
        acts[name[0]](int(name[1]))


    @pl.loop(0, 8)
    def _(i):
        here = pl.ds(pl.multiple_of(128 * i, 128), 128)
        value = proj[here, :]
        high, low = split(value)
        right_hi[here, :] = high
        right_lo[here, :] = low
        high, low = split(value.T)
        left_hi[:, here] = high
        left_lo[:, here] = low

    high, low = split(proj[1024:ROWS, :])
    right_hi[1024:ROWS, :] = high
    right_lo[1024:ROWS, :] = low

    def half_gram(half, g):
        rows = pl.ds(pl.multiple_of(256 * half, 256), 256)
        there = slice(32 * g, 32 * g + 1024)
        total = dot(left_hi[rows, :], right_hi[there, :])
        total += dot(left_lo[rows, :], right_hi[there, :])
        total += dot(left_hi[rows, :], right_lo[there, :])
        return total


    def core_sum(g):
        return remote(gram_out.at[g], gram_in.at[g], cs_s.at[g], cs_r.at[g], device(x, y, z, 1 - core))

    def to_plane(g, d):
        tx = around(x, lax.div(d, 4), 4)
        ty = around(y, lax.rem(d, 4), 4)
        src = gram.at[g, pl.ds(pl.multiple_of(64 * ty + 16 * tx, 16), 16), :]
        slot = 15 * g + d - 1
        return remote(src, plane.at[g, x, y], pl_s.at[slot], pl_r.at[slot], device(tx, ty, z, core))

    def half_rows(ty, half):
        return pl.ds(pl.multiple_of(64 * ty + 32 * half, 32), 32)

    def to_via(g, half):
        src = gram.at[g, half_rows(around(y, 2, 4), half), :]
        to = device(x, around(y, (1, 3)[half], 4), z, core)
        return remote(src, via.at[g, half], via_s.at[2 * g + half], via_r.at[2 * g + half], to)

    def place(tx, dy):
        return 4 * lax.rem(tx - x + 4, 4) + dy

    def all_planes(act):
        for dy in (0, 1, 3):
            @pl.loop(1 if dy == 0 else 0, 4)
            def _(k):
                act(4 * k + dy)

    def give_half(g):
        gram_out[g] = half_gram(1 - core, g)
        core_sum(g).start()
        drains.append(lambda: core_sum(g).wait_send())

    def give_plane(g):
        core_sum(g).wait_recv()
        gram[g] += gram_in[g]

        for half in (0, 1):
            to_via(g, half).start()

        @pl.loop(1, 4)
        def _(k):
            to_plane(g, 4 * k).start()

        for tx in (2, 3):
            to_plane(g, place(tx, 1)).start()
        for tx in (0, 1):
            to_plane(g, place(tx, 3)).start()

        plane[g, x, y] = gram[g, pl.ds(pl.multiple_of(64 * y + 16 * x, 16), 16), :]

        def drain():
            for half in (0, 1):
                to_via(g, half).wait_send()

        drains.append(drain)

    def give_rest(g):
        for half in (0, 1):
            dy = (1, 3)[half]
            to_via(g, half).wait_recv()
            gram[g, half_rows(around(y, dy, 4), half), :] += via[g, half]
            for k in (0, 1):
                to_plane(g, place(2 * half + k, dy)).start()
        drains.append(lambda: all_planes(lambda d: to_plane(g, d).wait_send()))

    give_half(0)
    gram[0] = half_gram(core, 0)
    give_half(1)
    give_plane(0)
    gram[1] = half_gram(core, 1)
    give_plane(1)
    give_rest(0)
    give_rest(1)

    def tile(t):
        return (slice(8 * (t // 4), 8 * (t // 4) + 8), slice(128 * (t % 4), 128 * (t % 4) + 128))

    def scatter(d):
        to = around(z, d, NZ)
        return remote(tiles_out.at[to], tiles_in.at[z], e1_s.at[d - 1], e1_r.at[d - 1], device(x, y, to, core))

    def bring_back(d):
        to = around(z, d, NZ)
        return remote(before_out.at[to], before_in.at[z], e2_s.at[d - 1], e2_r.at[d - 1], device(x, y, to, core))

    def apart(k):
        half = lax.div(k + 1, 2)
        return jnp.where(lax.rem(k, 2) == 1, half, -half)

    def owners(g, act):
        @pl.loop(0, NZ // 2)
        def _(k):
            d = lax.rem(NZ // 2 - lax.rem(g + z, 2) + 2 * apart(k), NZ)

            @pl.when(d > 0)
            def _():
                act(d)

    def give_tiles(g):
        all_planes(lambda d: to_plane(g, d).wait_recv())
        state = None
        for i in range(4):
            term = plane[g, i, y] + (plane[g, i, around(y, 1, 4)] + plane[g, i, around(y, 3, 4)])
            state = term if state is None else state + term
            states[i, g] = state
        for t in range(NZ // 2):
            tiles_out[2 * t + g] = states[(3, g) + tile(t)]
        owners(g, lambda d: scatter(d).start())

    def give_before(g):
        @pl.when(lax.rem(z, 2) == g)
        def _():
            tiles_in[z] = tiles_out[z]

            @pl.loop(1, NZ)
            def _(d):
                scatter(d).wait_recv()

            running = jnp.zeros((8, 128), F32)
            for t in range(NZ):
                before_out[t] = running
                running = running + tiles_in[t]

            @pl.loop(0, NZ - 1)
            def _(k):
                bring_back(NZ // 2 + apart(k)).start()

            before_in[z] = before_out[z]

    own_rows = pl.ds(pl.multiple_of(16 * x, 16), 16)

    def to_owner(i, g):
        to = device(2 * lax.div(i, 2) + core, y, z, lax.rem(i, 2))
        here = out.at[0, g, own_rows, :]
        return remote(final.at[i, g], here, f_s.at[4 * g + i], f_r.at[4 * g + x], to)

    def mine(i):
        return jnp.logical_and(x == 2 * lax.div(i, 2) + core, core == lax.rem(i, 2))

    def give_means(g):
        def arrived(d):
            bring_back(NZ - d).wait_recv()

        owners(g, arrived)
        for k in range(4):
            i = lax.rem(2 * (1 - x_hi) + k, 4)
            count = ((4 * z + i + 1) * (LAG_DEV * P_SIZE)).astype(F32)
            for t in range(NZ // 2):
                final[(i, g) + tile(t)] = (before_in[2 * t + g] + states[(i, g) + tile(t)]) / count

            @pl.when(mine(i))
            def _():
                out[0, g, own_rows, :] = final[i, g]

            @pl.when(jnp.logical_not(mine(i)))
            def _():
                to_owner(i, g).start()

            when_drain(jnp.logical_not(mine(i)), functools.partial(to_owner, i, g))

    def take_means(g):
        for i in range(4):
            @pl.when(jnp.logical_not(jnp.logical_and(x == i, core == x_lo)))
            def _():
                here = out.at[0, g, pl.ds(16 * i, 16), :]
                at = 4 * g + i
                remote(final.at[0, g], here, f_s.at[at], f_r.at[at], device(x, y, z, 1 - core)).wait_recv()

    for act in (give_tiles, give_before, give_means, take_means):
        for g in (0, 1):
            act(g)

    def sent_along_z():
        @pl.loop(1, NZ)
        def _(d):
            scatter(d).wait_send()

    def sent_back():
        @pl.loop(1, NZ)
        def _(d):
            bring_back(d).wait_send()

    drains += [sent_along_z, sent_back]

    for act in drains:
        act()


def body(markov, basis):
    vmem = pl.BlockSpec(memory_space=pltpu.VMEM)
    hbm = pl.BlockSpec(memory_space=pltpu.HBM)
    counts = [15, 15, 24, 24, 24, 24, 8, 8, 2, 2, 4, 4, 30, 30, 15, 15, 15, 15, 8, 8, 2]
    return pl.pallas_call(
        kernel,
        out_shape=jax.ShapeDtypeStruct((1, 2, 64, 512), F32),
        in_specs=[hbm, hbm],
        out_specs=vmem,
        scratch_shapes=[
            pltpu.VMEM((32, 32, 64), F32),
            pltpu.VMEM((16, 32, 128), F32),
            pltpu.VMEM((2, 16, 32, 128), F32),
            pltpu.VMEM((2080, 768), BF16),
            pltpu.VMEM((16, 2, 2, 4, 8, 512), F32),
            pltpu.VMEM((768, 512), BF16),
            pltpu.VMEM((ROWS, 512), F32),
            pltpu.VMEM((ROWS, 512), BF16),
            pltpu.VMEM((ROWS, 512), BF16),
            pltpu.VMEM((512, 1024), BF16),
            pltpu.VMEM((512, 1024), BF16),
            pltpu.VMEM((2, 256, 512), F32),
            pltpu.VMEM((2, 256, 512), F32),
            pltpu.VMEM((2, 256, 512), F32),
            pltpu.VMEM((2, 2, 32, 512), F32),
            pltpu.VMEM((2, 4, 4, 16, 512), F32),
            pltpu.VMEM((4, 2, 16, 512), F32),
            pltpu.VMEM((NZ, 8, 128), F32),
            pltpu.VMEM((NZ, 8, 128), F32),
            pltpu.VMEM((NZ, 8, 128), F32),
            pltpu.VMEM((NZ, 8, 128), F32),
            pltpu.VMEM((4, 2, 16, 512), F32),
        ]
        + [pltpu.SemaphoreType.DMA((2, 4))] * 2
        + [pltpu.SemaphoreType.DMA((n,)) for n in counts],
        compiler_params=pltpu.CompilerParams(
            collective_id=0, has_side_effects=True, vmem_limit_bytes=62 * 1024 * 1024
        ),
        cost_estimate=pl.CostEstimate(flops=10_000_000_000, bytes_accessed=1_000_000, transcendentals=0),
    )(markov, basis)


def solution(mesh):
    placed = (P("lag", "out", None), P("lag", None))
    return jax.shard_map(
        body, mesh=mesh, in_specs=placed, out_specs=P("lag", None, "out", None), check_vma=False
    )
```

```python
import functools

import jax
import jax.numpy as jnp
from jax import lax
from jax.experimental import pallas as pl
from jax.experimental.pallas import tpu as pltpu
from jax.sharding import PartitionSpec as P

P_SIZE = 256
LAG_DEV = 32
MESH = pl.DeviceIdType.MESH
F32 = jnp.float32
BF16 = jnp.bfloat16

NZ = 16
CHUNKS = 8
X_LAST = (0, 1, 2, 3, 4, 5, 6, 7)
ORDER = (
    "M0", "M1", "A0", "M2", "A1", "M3", "A2", "A3", "B0", "A4", "B1", "B2", "A5", "A6", "B3", "B4", "L0", "A7", "B5", "C0",
    "B6", "C1", "D0", "C2", "D1", "C3", "B7", "D2", "C4", "D3", "C5", "D4", "C6", "D5", "C7", "D6", "D7",
)
ROWS = 1056
TILE_M = 528


def split(value):
    high = value.astype(BF16)
    low = (value - high.astype(F32)).astype(BF16)
    return high, low


def device(x, y, z, core):
    return (4 * z + 2 * lax.div(x, 2) + core, 4 * lax.rem(x, 2) + y)


def dot(a, b):
    return jnp.dot(a, b, preferred_element_type=F32)


def kernel(
    markov_hbm, basis, out,
    markov, packed, pairs, lhs, gathered, weights, proj, right_hi, right_lo, left_hi, left_lo,
    gram_out, gram_in, gram, via, plane, states, tiles_out, tiles_in, before_out, before_in, final,
    mk_s, mk_r, b1_s, b1_r, b2_s, b2_r, b3_s, b3_r, b4_s, b4_r, cs_s, cs_r, via_s, via_r, pl_s, pl_r,
    e1_s, e1_r, e2_s, e2_r, f_s, f_r, in_s,
):
    lag = lax.axis_index("lag")
    chan = lax.axis_index("out")
    z = lax.div(lag, 4)
    x_hi = lax.rem(lax.div(lag, 2), 2)
    core = lax.rem(lag, 2)
    x_lo = lax.div(chan, 4)
    y = lax.rem(chan, 4)
    x = 2 * x_hi + x_lo
    block = 4 * z + x
    swapped = core != x_lo

    def remote(src, dst, send, recv, to):
        return pltpu.make_async_remote_copy(
            src_ref=src, dst_ref=dst, send_sem=send, recv_sem=recv, device_id=to, device_id_type=MESH
        )

    def around(value, step, size):
        return lax.rem(value + step, size)

    rows8 = pl.ds(pl.multiple_of(8 * y, 8), 8)
    cols = pl.ds(pl.multiple_of(256 * x_lo, 256), 256)
    take_markov = pltpu.make_async_copy(markov_hbm, markov, in_s.at[0])
    take_basis = pltpu.make_async_copy(
        basis.at[rows8, cols], gathered.at[z, x_hi, core, y, :, cols], in_s.at[1]
    )
    take_markov.start()
    take_basis.start()

    drains = []

    def loop_drain(make, count):
        def act():
            @pl.loop(1, count)
            def _(d):
                make(d).wait_send()

        drains.append(act)

    def when_drain(condition, make):
        def act():
            @pl.when(condition)
            def _():
                make().wait_send()

        drains.append(act)

    barrier = pltpu.get_barrier_semaphore()

    def greet(to):
        pl.semaphore_signal(barrier, inc=1, device_id=to, device_id_type=MESH)

    @pl.loop(1, NZ)
    def _(d):
        greet(device(x, y, around(z, d, NZ), core))

    @pl.loop(1, 16)
    def _(d):
        greet(device(around(x, lax.div(d, 4), 4), around(y, lax.rem(d, 4), 4), z, core))

    @pl.loop(0, 4)
    def _(d):
        greet(device(around(x, d, 4), y, z, 1 - core))

    gives_down = jnp.logical_and(lax.rem(lag, 4) == 0, z > 0)
    takes_up = jnp.logical_and(x == 3, z < NZ - 1)

    @pl.when(gives_down)
    def _():
        greet(device(3, y, z - 1, x_lo))

    @pl.when(takes_up)
    def _():
        greet((4 * (z + 1), 4 * core + y))

    take_markov.wait()
    for t in range(LAG_DEV // 2):
        packed[t] = jnp.concatenate([markov[2 * t], markov[2 * t + 1]], axis=-1)

    take_basis.wait()
    pl.semaphore_wait(barrier, 34 + gives_down.astype(jnp.int32) + takes_up.astype(jnp.int32))


    def level1(d, zz):
        piece = gathered.at[zz, x_hi, core, y, :, cols]
        return remote(piece, piece, b1_s.at[d - 1], b1_r.at[d - 1], device(x, y, around(z, d, NZ), core))

    @pl.loop(0, NZ - 1)
    def _(k):
        near = lax.div(k, 2)
        level1(jnp.where(lax.rem(k, 2) == 0, near + 1, NZ - 1 - near), z).start()

    loop_drain(lambda d: level1(d, z), NZ)

    def to_block(i):
        part = pl.ds(4 * i, 4)
        to = device(2 * x_hi + core, y, z, x_lo)
        return remote(packed.at[part], pairs.at[0, part], mk_s.at[0, i], mk_r.at[0, i], to)

    def to_before(i):
        part = pl.ds(4 * i, 4)
        earlier = lag - 1
        to = device(lax.rem(earlier, 4), y, lax.div(earlier, 4), x_lo)
        return remote(packed.at[part], pairs.at[1, part], mk_s.at[1, i], mk_r.at[1, i], to)

    def give_quarter(i):
        @pl.when(swapped)
        def _():
            to_block(i).start()

        @pl.when(lag > 0)
        def _():
            to_before(i).start()

        when_drain(swapped, functools.partial(to_block, i))
        when_drain(lag > 0, functools.partial(to_before, i))

    @pl.when(jnp.logical_not(swapped))
    def _():
        pairs[0] = packed[...]

    @pl.when(block == 4 * NZ - 1)
    def _():
        pairs[1] = jnp.zeros_like(packed)

    def chunk_of(q):
        away = (q + 1) // 2 if q % 2 else CHUNKS - q // 2
        return lax.rem(lax.div(z, 2) + away, CHUNKS)

    def zs_of(q):
        return pl.ds(2 * chunk_of(q), 2)

    def wait_level1(q):
        @pl.loop(0, 2)
        def _(i):
            source = 2 * chunk_of(q) + i
            d = lax.rem(z - source + NZ, NZ)

            @pl.when(d > 0)
            def _():
                level1(d, source).wait_recv()

    def level2(q, d):
        piece = gathered.at[zs_of(q), x_hi, core, y, :, cols]
        x_next, y_next = device(around(x, d, 4), y, z, core), device(x, around(y, d, 4), z, core)
        if q in X_LAST:
            to = tuple(jnp.where(core == 0, b, a) for a, b in zip(x_next, y_next))
        else:
            to = x_next
        slot = 3 * q + d - 1
        return remote(piece, piece, b2_s.at[slot], b2_r.at[slot], to)

    def level3(q, d, x_last):
        slot = 3 * q + d - 1
        if x_last:
            piece = gathered.at[zs_of(q), x_hi, core, :, :, cols]
            to = device(around(x, d, 4), y, z, core)
        else:
            piece = gathered.at[zs_of(q), :, core, y]
            to = device(x, around(y, d, 4), z, core)
        return remote(piece, piece, b3_s.at[slot], b3_r.at[slot], to)

    def by_order(q, act):
        if q not in X_LAST:
            act(False)
            return

        for x_last in (True, False):
            @pl.when((core == 0) == x_last)
            def _():
                act(x_last)

    def level4(q):
        piece = gathered.at[zs_of(q), :, core]
        return remote(piece, piece, b4_s.at[q], b4_r.at[q], device(x, y, z, 1 - core))

    def wait2_start3(q):
        for d in (1, 2, 3):
            level2(q, d).wait_recv()

        def act(x_last):
            for d in (1, 2, 3):
                level3(q, d, x_last).start()

        def drain(x_last):
            for d in (1, 2, 3):
                level3(q, d, x_last).wait_send()

        by_order(q, act)
        drains.append(lambda: by_order(q, drain))

    def wait3_start4(q):
        def act(x_last):
            for d in (1, 2, 3):
                level3(q, d, x_last).wait_recv()

        by_order(q, act)
        level4(q).start()
        drains.append(lambda: level4(q).wait_send())

    def wait1_start2(q):
        wait_level1(q)
        for d in (1, 2, 3):
            level2(q, d).start()

        def drain():
            for d in (1, 2, 3):
                level2(q, d).wait_send()

        drains.append(drain)

    def build_lhs(_):
        proj[...] = jnp.zeros_like(proj)

        @pl.when(swapped)
        def _():
            for i in range(4):
                to_block(i).wait_recv()

        @pl.when(block < 4 * NZ - 1)
        def _():
            for i in range(4):
                to_before(i).wait_recv()

        first_half = lax.broadcasted_iota(jnp.int32, (32, 128), 1) < 64

        def put(t, value):
            high, low = split(value)
            for place, part in ((0, high), (256, low), (512, high)):
                lhs[pl.ds(pl.multiple_of(32 * t + 64, 32), 32), place : place + 128] = part
                lhs[pl.ds(pl.multiple_of(32 * t, 32), 32), place + 128 : place + 256] = part

        def both(t, this, following):
            put(2 * t, this)
            put(2 * t + 1, jnp.where(first_half, pltpu.roll(this, 64, 1), pltpu.roll(following, 64, 1)))

        for side in (0, 1):
            @pl.loop(0, 15)
            def _(t):
                both(16 * side + t, pairs[side, t], pairs[side, t + 1])

        both(15, pairs[0, 15], pairs[1, 0])
        put(62, pairs[1, 15])

    def compute(q):
        level4(q).wait_recv()

        part = chunk_of(q)
        for i in range(2):
            for h in range(2):
                for w in range(2):
                    high, low = split(gathered[2 * part + i, h, w].reshape(32, 512))
                    at = 128 * i + 64 * h + 32 * w
                    weights[at : at + 32, :] = high
                    weights[256 + at : 288 + at, :] = high
                    weights[512 + at : 544 + at, :] = low

        @pl.loop(0, ROWS // TILE_M)
        def _(m):
            here = pl.ds(pl.multiple_of(TILE_M * m, 16), TILE_M)
            there = pl.ds(pl.multiple_of(128 * part + 64 + TILE_M * m, 16), TILE_M)
            proj[here, :] += dot(lhs[there, :], weights[...])


    acts = dict(M=give_quarter, L=build_lhs, A=wait1_start2, B=wait2_start3, C=wait3_start4, D=compute)
    for name in ORDER:
        acts[name[0]](int(name[1]))


    @pl.loop(0, 8)
    def _(i):
        here = pl.ds(pl.multiple_of(128 * i, 128), 128)
        value = proj[here, :]
        high, low = split(value)
        right_hi[here, :] = high
        right_lo[here, :] = low
        high, low = split(value.T)
        left_hi[:, here] = high
        left_lo[:, here] = low

    high, low = split(proj[1024:ROWS, :])
    right_hi[1024:ROWS, :] = high
    right_lo[1024:ROWS, :] = low

    def half_gram(half, g):
        rows = pl.ds(pl.multiple_of(256 * half, 256), 256)
        there = slice(32 * g, 32 * g + 1024)
        total = dot(left_hi[rows, :], right_hi[there, :])
        total += dot(left_lo[rows, :], right_hi[there, :])
        total += dot(left_hi[rows, :], right_lo[there, :])
        return total


    def core_sum(g):
        return remote(gram_out.at[g], gram_in.at[g], cs_s.at[g], cs_r.at[g], device(x, y, z, 1 - core))

    def to_plane(g, d):
        tx = around(x, lax.div(d, 4), 4)
        ty = around(y, lax.rem(d, 4), 4)
        src = gram.at[g, pl.ds(pl.multiple_of(64 * ty + 16 * tx, 16), 16), :]
        slot = 15 * g + d - 1
        return remote(src, plane.at[g, x, y], pl_s.at[slot], pl_r.at[slot], device(tx, ty, z, core))

    def half_rows(ty, half):
        return pl.ds(pl.multiple_of(64 * ty + 32 * half, 32), 32)

    def to_via(g, half):
        src = gram.at[g, half_rows(around(y, 2, 4), half), :]
        to = device(x, around(y, (1, 3)[half], 4), z, core)
        return remote(src, via.at[g, half], via_s.at[2 * g + half], via_r.at[2 * g + half], to)

    def place(tx, dy):
        return 4 * lax.rem(tx - x + 4, 4) + dy

    def all_planes(act):
        for dy in (0, 1, 3):
            @pl.loop(1 if dy == 0 else 0, 4)
            def _(k):
                act(4 * k + dy)

    def give_half(g):
        gram_out[g] = half_gram(1 - core, g)
        core_sum(g).start()
        drains.append(lambda: core_sum(g).wait_send())

    def give_plane(g):
        core_sum(g).wait_recv()
        gram[g] += gram_in[g]

        for half in (0, 1):
            to_via(g, half).start()

        @pl.loop(1, 4)
        def _(k):
            to_plane(g, 4 * k).start()

        for tx in (2, 3):
            to_plane(g, place(tx, 1)).start()
        for tx in (0, 1):
            to_plane(g, place(tx, 3)).start()

        plane[g, x, y] = gram[g, pl.ds(pl.multiple_of(64 * y + 16 * x, 16), 16), :]

        def drain():
            for half in (0, 1):
                to_via(g, half).wait_send()

        drains.append(drain)

    def give_rest(g):
        for half in (0, 1):
            dy = (1, 3)[half]
            to_via(g, half).wait_recv()
            gram[g, half_rows(around(y, dy, 4), half), :] += via[g, half]
            for k in (0, 1):
                to_plane(g, place(2 * half + k, dy)).start()
        drains.append(lambda: all_planes(lambda d: to_plane(g, d).wait_send()))

    give_half(0)
    gram[0] = half_gram(core, 0)
    give_half(1)
    give_plane(0)
    gram[1] = half_gram(core, 1)
    give_plane(1)
    give_rest(0)
    give_rest(1)

    def tile(t):
        return (slice(8 * (t // 4), 8 * (t // 4) + 8), slice(128 * (t % 4), 128 * (t % 4) + 128))

    def scatter(d):
        to = around(z, d, NZ)
        return remote(tiles_out.at[to], tiles_in.at[z], e1_s.at[d - 1], e1_r.at[d - 1], device(x, y, to, core))

    def bring_back(d):
        to = around(z, d, NZ)
        return remote(before_out.at[to], before_in.at[z], e2_s.at[d - 1], e2_r.at[d - 1], device(x, y, to, core))

    def apart(k):
        half = lax.div(k + 1, 2)
        return jnp.where(lax.rem(k, 2) == 1, half, -half)

    def owners(g, act):
        @pl.loop(0, NZ // 2)
        def _(k):
            d = lax.rem(NZ // 2 - lax.rem(g + z, 2) + 2 * apart(k), NZ)

            @pl.when(d > 0)
            def _():
                act(d)

    def give_tiles(g):
        all_planes(lambda d: to_plane(g, d).wait_recv())
        state = None
        for i in range(4):
            term = plane[g, i, y] + (plane[g, i, around(y, 1, 4)] + plane[g, i, around(y, 3, 4)])
            state = term if state is None else state + term
            states[i, g] = state
        for t in range(NZ // 2):
            tiles_out[2 * t + g] = states[(3, g) + tile(t)]
        owners(g, lambda d: scatter(d).start())

    def give_before(g):
        @pl.when(lax.rem(z, 2) == g)
        def _():
            tiles_in[z] = tiles_out[z]

            @pl.loop(1, NZ)
            def _(d):
                scatter(d).wait_recv()

            running = jnp.zeros((8, 128), F32)
            for t in range(NZ):
                before_out[t] = running
                running = running + tiles_in[t]

            @pl.loop(0, NZ - 1)
            def _(k):
                bring_back(NZ // 2 + apart(k)).start()

            before_in[z] = before_out[z]

    own_rows = pl.ds(pl.multiple_of(16 * x, 16), 16)

    def to_owner(i, g):
        to = device(2 * lax.div(i, 2) + core, y, z, lax.rem(i, 2))
        here = out.at[0, g, own_rows, :]
        return remote(final.at[i, g], here, f_s.at[4 * g + i], f_r.at[4 * g + x], to)

    def mine(i):
        return jnp.logical_and(x == 2 * lax.div(i, 2) + core, core == lax.rem(i, 2))

    def give_means(g):
        def arrived(d):
            bring_back(NZ - d).wait_recv()

        owners(g, arrived)
        for k in range(4):
            i = lax.rem(2 * (1 - x_hi) + k, 4)
            count = ((4 * z + i + 1) * (LAG_DEV * P_SIZE)).astype(F32)
            for t in range(NZ // 2):
                final[(i, g) + tile(t)] = (before_in[2 * t + g] + states[(i, g) + tile(t)]) / count

            @pl.when(mine(i))
            def _():
                out[0, g, own_rows, :] = final[i, g]

            @pl.when(jnp.logical_not(mine(i)))
            def _():
                to_owner(i, g).start()

            when_drain(jnp.logical_not(mine(i)), functools.partial(to_owner, i, g))

    def take_means(g):
        for i in range(4):
            @pl.when(jnp.logical_not(jnp.logical_and(x == i, core == x_lo)))
            def _():
                here = out.at[0, g, pl.ds(16 * i, 16), :]
                at = 4 * g + i
                remote(final.at[0, g], here, f_s.at[at], f_r.at[at], device(x, y, z, 1 - core)).wait_recv()

    def wait_sent():
        for act in drains:
            act()
        drains.clear()

    for g in (0, 1):
        give_tiles(g)
    wait_sent()
    for g in (0, 1):
        give_before(g)

    @pl.loop(1, NZ)
    def _(d):
        scatter(d).wait_send()

    for g in (0, 1):
        give_means(g)

    @pl.loop(1, NZ)
    def _(d):
        bring_back(d).wait_send()

    for g in (0, 1):
        take_means(g)
    wait_sent()


def body(markov, basis):
    vmem = pl.BlockSpec(memory_space=pltpu.VMEM)
    hbm = pl.BlockSpec(memory_space=pltpu.HBM)
    counts = [15, 15, 24, 24, 24, 24, 8, 8, 2, 2, 4, 4, 30, 30, 15, 15, 15, 15, 8, 8, 2]
    return pl.pallas_call(
        kernel,
        out_shape=jax.ShapeDtypeStruct((1, 2, 64, 512), F32),
        in_specs=[hbm, hbm],
        out_specs=vmem,
        scratch_shapes=[
            pltpu.VMEM((32, 32, 64), F32),
            pltpu.VMEM((16, 32, 128), F32),
            pltpu.VMEM((2, 16, 32, 128), F32),
            pltpu.VMEM((2080, 768), BF16),
            pltpu.VMEM((16, 2, 2, 4, 8, 512), F32),
            pltpu.VMEM((768, 512), BF16),
            pltpu.VMEM((ROWS, 512), F32),
            pltpu.VMEM((ROWS, 512), BF16),
            pltpu.VMEM((ROWS, 512), BF16),
            pltpu.VMEM((512, 1024), BF16),
            pltpu.VMEM((512, 1024), BF16),
            pltpu.VMEM((2, 256, 512), F32),
            pltpu.VMEM((2, 256, 512), F32),
            pltpu.VMEM((2, 256, 512), F32),
            pltpu.VMEM((2, 2, 32, 512), F32),
            pltpu.VMEM((2, 4, 4, 16, 512), F32),
            pltpu.VMEM((4, 2, 16, 512), F32),
            pltpu.VMEM((NZ, 8, 128), F32),
            pltpu.VMEM((NZ, 8, 128), F32),
            pltpu.VMEM((NZ, 8, 128), F32),
            pltpu.VMEM((NZ, 8, 128), F32),
            pltpu.VMEM((4, 2, 16, 512), F32),
        ]
        + [pltpu.SemaphoreType.DMA((2, 4))] * 2
        + [pltpu.SemaphoreType.DMA((n,)) for n in counts],
        compiler_params=pltpu.CompilerParams(
            collective_id=0, has_side_effects=True, vmem_limit_bytes=62 * 1024 * 1024
        ),
        cost_estimate=pl.CostEstimate(flops=10_000_000_000, bytes_accessed=1_000_000, transcendentals=0),
    )(markov, basis)


def solution(mesh):
    placed = (P("lag", "out", None), P("lag", None))
    return jax.shard_map(
        body, mesh=mesh, in_specs=placed, out_specs=P("lag", None, "out", None), check_vma=False
    )
```

```python
import functools

import jax
import jax.numpy as jnp
from jax import lax
from jax.experimental import pallas as pl
from jax.experimental.pallas import tpu as pltpu
from jax.sharding import PartitionSpec as P

P_SIZE = 256
LAG_DEV = 32
MESH = pl.DeviceIdType.MESH
F32 = jnp.float32
BF16 = jnp.bfloat16

NZ = 16
CHUNKS = 8
X_LAST = (0, 1, 2, 3, 4, 5, 6, 7)
ORDER = (
    "M0", "M1", "A0", "M2", "A1", "M3", "A2", "A3", "B0", "A4", "B1", "B2", "A5", "A6", "B3", "B4", "L0", "A7", "B5", "C0",
    "B6", "C1", "D0", "C2", "D1", "C3", "B7", "D2", "C4", "D3", "C5", "D4", "C6", "D5", "C7", "D6", "D7",
)
ROWS = 1056
TILE_M = 1056


def split(value):
    high = value.astype(BF16)
    low = (value - high.astype(F32)).astype(BF16)
    return high, low


def device(x, y, z, core):
    return (4 * z + 2 * lax.div(x, 2) + core, 4 * lax.rem(x, 2) + y)


def dot(a, b):
    return jnp.dot(a, b, preferred_element_type=F32)


def kernel(
    markov_hbm, basis, out,
    markov, packed, pairs, lhs, gathered, weights, proj, right_hi, right_lo, left_hi, left_lo,
    gram_out, gram_in, gram, via, plane, states, tiles_out, tiles_in, before_out, before_in, final,
    mk_s, mk_r, b1_s, b1_r, b2_s, b2_r, b3_s, b3_r, b4_s, b4_r, cs_s, cs_r, via_s, via_r, pl_s, pl_r,
    e1_s, e1_r, e2_s, e2_r, f_s, f_r, in_s,
):
    lag = lax.axis_index("lag")
    chan = lax.axis_index("out")
    z = lax.div(lag, 4)
    x_hi = lax.rem(lax.div(lag, 2), 2)
    core = lax.rem(lag, 2)
    x_lo = lax.div(chan, 4)
    y = lax.rem(chan, 4)
    x = 2 * x_hi + x_lo
    block = 4 * z + x
    swapped = core != x_lo

    def remote(src, dst, send, recv, to):
        return pltpu.make_async_remote_copy(
            src_ref=src, dst_ref=dst, send_sem=send, recv_sem=recv, device_id=to, device_id_type=MESH
        )

    def around(value, step, size):
        return lax.rem(value + step, size)

    rows8 = pl.ds(pl.multiple_of(8 * y, 8), 8)
    cols = pl.ds(pl.multiple_of(256 * x_lo, 256), 256)
    take_markov = pltpu.make_async_copy(markov_hbm, markov, in_s.at[0])
    take_basis = pltpu.make_async_copy(
        basis.at[rows8, cols], gathered.at[z, x_hi, core, y, :, cols], in_s.at[1]
    )
    take_markov.start()
    take_basis.start()

    drains = []

    def loop_drain(make, count):
        def act():
            @pl.loop(1, count)
            def _(d):
                make(d).wait_send()

        drains.append(act)

    def when_drain(condition, make):
        def act():
            @pl.when(condition)
            def _():
                make().wait_send()

        drains.append(act)

    barrier = pltpu.get_barrier_semaphore()

    def greet(to):
        pl.semaphore_signal(barrier, inc=1, device_id=to, device_id_type=MESH)

    @pl.loop(1, NZ)
    def _(d):
        greet(device(x, y, around(z, d, NZ), core))

    @pl.loop(1, 16)
    def _(d):
        greet(device(around(x, lax.div(d, 4), 4), around(y, lax.rem(d, 4), 4), z, core))

    @pl.loop(0, 4)
    def _(d):
        greet(device(around(x, d, 4), y, z, 1 - core))

    gives_down = jnp.logical_and(lax.rem(lag, 4) == 0, z > 0)
    takes_up = jnp.logical_and(x == 3, z < NZ - 1)

    @pl.when(gives_down)
    def _():
        greet(device(3, y, z - 1, x_lo))

    @pl.when(takes_up)
    def _():
        greet((4 * (z + 1), 4 * core + y))

    take_markov.wait()
    for t in range(LAG_DEV // 2):
        packed[t] = jnp.concatenate([markov[2 * t], markov[2 * t + 1]], axis=-1)

    take_basis.wait()
    pl.semaphore_wait(barrier, 34 + gives_down.astype(jnp.int32) + takes_up.astype(jnp.int32))


    def level1(d, zz):
        piece = gathered.at[zz, x_hi, core, y, :, cols]
        return remote(piece, piece, b1_s.at[d - 1], b1_r.at[d - 1], device(x, y, around(z, d, NZ), core))

    @pl.loop(0, NZ - 1)
    def _(k):
        near = lax.div(k, 2)
        level1(jnp.where(lax.rem(k, 2) == 0, near + 1, NZ - 1 - near), z).start()

    loop_drain(lambda d: level1(d, z), NZ)

    def to_block(i):
        part = pl.ds(4 * i, 4)
        to = device(2 * x_hi + core, y, z, x_lo)
        return remote(packed.at[part], pairs.at[0, part], mk_s.at[0, i], mk_r.at[0, i], to)

    def to_before(i):
        part = pl.ds(4 * i, 4)
        earlier = lag - 1
        to = device(lax.rem(earlier, 4), y, lax.div(earlier, 4), x_lo)
        return remote(packed.at[part], pairs.at[1, part], mk_s.at[1, i], mk_r.at[1, i], to)

    def give_quarter(i):
        @pl.when(swapped)
        def _():
            to_block(i).start()

        @pl.when(lag > 0)
        def _():
            to_before(i).start()

        when_drain(swapped, functools.partial(to_block, i))
        when_drain(lag > 0, functools.partial(to_before, i))

    @pl.when(jnp.logical_not(swapped))
    def _():
        pairs[0] = packed[...]

    @pl.when(block == 4 * NZ - 1)
    def _():
        pairs[1] = jnp.zeros_like(packed)

    def chunk_of(q):
        away = (q + 1) // 2 if q % 2 else CHUNKS - q // 2
        return lax.rem(lax.div(z, 2) + away, CHUNKS)

    def zs_of(q):
        return pl.ds(2 * chunk_of(q), 2)

    def wait_level1(q):
        @pl.loop(0, 2)
        def _(i):
            source = 2 * chunk_of(q) + i
            d = lax.rem(z - source + NZ, NZ)

            @pl.when(d > 0)
            def _():
                level1(d, source).wait_recv()

    def level2(q, d):
        piece = gathered.at[zs_of(q), x_hi, core, y, :, cols]
        x_next, y_next = device(around(x, d, 4), y, z, core), device(x, around(y, d, 4), z, core)
        if q in X_LAST:
            to = tuple(jnp.where(core == 0, b, a) for a, b in zip(x_next, y_next))
        else:
            to = x_next
        slot = 3 * q + d - 1
        return remote(piece, piece, b2_s.at[slot], b2_r.at[slot], to)

    def level3(q, d, x_last):
        slot = 3 * q + d - 1
        if x_last:
            piece = gathered.at[zs_of(q), x_hi, core, :, :, cols]
            to = device(around(x, d, 4), y, z, core)
        else:
            piece = gathered.at[zs_of(q), :, core, y]
            to = device(x, around(y, d, 4), z, core)
        return remote(piece, piece, b3_s.at[slot], b3_r.at[slot], to)

    def by_order(q, act):
        if q not in X_LAST:
            act(False)
            return

        for x_last in (True, False):
            @pl.when((core == 0) == x_last)
            def _():
                act(x_last)

    def level4(q):
        piece = gathered.at[zs_of(q), :, core]
        return remote(piece, piece, b4_s.at[q], b4_r.at[q], device(x, y, z, 1 - core))

    def wait2_start3(q):
        for d in (1, 2, 3):
            level2(q, d).wait_recv()

        def act(x_last):
            for d in (1, 2, 3):
                level3(q, d, x_last).start()

        def drain(x_last):
            for d in (1, 2, 3):
                level3(q, d, x_last).wait_send()

        by_order(q, act)
        drains.append(lambda: by_order(q, drain))

    def wait3_start4(q):
        def act(x_last):
            for d in (1, 2, 3):
                level3(q, d, x_last).wait_recv()

        by_order(q, act)
        level4(q).start()
        drains.append(lambda: level4(q).wait_send())

    def wait1_start2(q):
        wait_level1(q)
        for d in (1, 2, 3):
            level2(q, d).start()

        def drain():
            for d in (1, 2, 3):
                level2(q, d).wait_send()

        drains.append(drain)

    def build_lhs(_):
        proj[...] = jnp.zeros_like(proj)

        @pl.when(swapped)
        def _():
            for i in range(4):
                to_block(i).wait_recv()

        @pl.when(block < 4 * NZ - 1)
        def _():
            for i in range(4):
                to_before(i).wait_recv()

        first_half = lax.broadcasted_iota(jnp.int32, (32, 128), 1) < 64

        def put(t, value):
            high, low = split(value)
            for place, part in ((0, high), (256, low), (512, high)):
                lhs[pl.ds(pl.multiple_of(32 * t + 64, 32), 32), place : place + 128] = part
                lhs[pl.ds(pl.multiple_of(32 * t, 32), 32), place + 128 : place + 256] = part

        def both(t, this, following):
            put(2 * t, this)
            put(2 * t + 1, jnp.where(first_half, pltpu.roll(this, 64, 1), pltpu.roll(following, 64, 1)))

        for side in (0, 1):
            @pl.loop(0, 15)
            def _(t):
                both(16 * side + t, pairs[side, t], pairs[side, t + 1])

        both(15, pairs[0, 15], pairs[1, 0])
        put(62, pairs[1, 15])

    def compute(q):
        level4(q).wait_recv()

        part = chunk_of(q)
        for i in range(2):
            for h in range(2):
                for w in range(2):
                    high, low = split(gathered[2 * part + i, h, w].reshape(32, 512))
                    at = 128 * i + 64 * h + 32 * w
                    weights[at : at + 32, :] = high
                    weights[256 + at : 288 + at, :] = high
                    weights[512 + at : 544 + at, :] = low

        @pl.loop(0, ROWS // TILE_M)
        def _(m):
            here = pl.ds(pl.multiple_of(TILE_M * m, 16), TILE_M)
            there = pl.ds(pl.multiple_of(128 * part + 64 + TILE_M * m, 16), TILE_M)
            proj[here, :] += dot(lhs[there, :], weights[...])


    acts = dict(M=give_quarter, L=build_lhs, A=wait1_start2, B=wait2_start3, C=wait3_start4, D=compute)
    for name in ORDER:
        acts[name[0]](int(name[1]))


    @pl.loop(0, 8)
    def _(i):
        here = pl.ds(pl.multiple_of(128 * i, 128), 128)
        value = proj[here, :]
        high, low = split(value)
        right_hi[here, :] = high
        right_lo[here, :] = low
        high, low = split(value.T)
        left_hi[:, here] = high
        left_lo[:, here] = low

    high, low = split(proj[1024:ROWS, :])
    right_hi[1024:ROWS, :] = high
    right_lo[1024:ROWS, :] = low

    def half_gram(half, g):
        rows = pl.ds(pl.multiple_of(256 * half, 256), 256)
        there = slice(32 * g, 32 * g + 1024)
        total = dot(left_hi[rows, :], right_hi[there, :])
        total += dot(left_lo[rows, :], right_hi[there, :])
        total += dot(left_hi[rows, :], right_lo[there, :])
        return total


    def core_sum(g):
        return remote(gram_out.at[g], gram_in.at[g], cs_s.at[g], cs_r.at[g], device(x, y, z, 1 - core))

    def to_plane(g, d):
        tx = around(x, lax.div(d, 4), 4)
        ty = around(y, lax.rem(d, 4), 4)
        src = gram.at[g, pl.ds(pl.multiple_of(64 * ty + 16 * tx, 16), 16), :]
        slot = 15 * g + d - 1
        return remote(src, plane.at[g, x, y], pl_s.at[slot], pl_r.at[slot], device(tx, ty, z, core))

    def half_rows(ty, half):
        return pl.ds(pl.multiple_of(64 * ty + 32 * half, 32), 32)

    def to_via(g, half):
        src = gram.at[g, half_rows(around(y, 2, 4), half), :]
        to = device(x, around(y, (1, 3)[half], 4), z, core)
        return remote(src, via.at[g, half], via_s.at[2 * g + half], via_r.at[2 * g + half], to)

    def place(tx, dy):
        return 4 * lax.rem(tx - x + 4, 4) + dy

    def all_planes(act):
        for dy in (0, 1, 3):
            @pl.loop(1 if dy == 0 else 0, 4)
            def _(k):
                act(4 * k + dy)

    def give_half(g):
        gram_out[g] = half_gram(1 - core, g)
        core_sum(g).start()
        drains.append(lambda: core_sum(g).wait_send())

    def give_plane(g):
        core_sum(g).wait_recv()
        gram[g] += gram_in[g]

        for half in (0, 1):
            to_via(g, half).start()

        @pl.loop(1, 4)
        def _(k):
            to_plane(g, 4 * k).start()

        for tx in (2, 3):
            to_plane(g, place(tx, 1)).start()
        for tx in (0, 1):
            to_plane(g, place(tx, 3)).start()

        plane[g, x, y] = gram[g, pl.ds(pl.multiple_of(64 * y + 16 * x, 16), 16), :]

        def drain():
            for half in (0, 1):
                to_via(g, half).wait_send()

        drains.append(drain)

    def give_rest(g):
        for half in (0, 1):
            dy = (1, 3)[half]
            to_via(g, half).wait_recv()
            gram[g, half_rows(around(y, dy, 4), half), :] += via[g, half]
            for k in (0, 1):
                to_plane(g, place(2 * half + k, dy)).start()
        drains.append(lambda: all_planes(lambda d: to_plane(g, d).wait_send()))

    give_half(0)
    gram[0] = half_gram(core, 0)
    give_half(1)
    give_plane(0)
    gram[1] = half_gram(core, 1)
    give_plane(1)
    give_rest(0)
    give_rest(1)

    def tile(t):
        return (slice(8 * (t // 4), 8 * (t // 4) + 8), slice(128 * (t % 4), 128 * (t % 4) + 128))

    def scatter(d):
        to = around(z, d, NZ)
        return remote(tiles_out.at[to], tiles_in.at[z], e1_s.at[d - 1], e1_r.at[d - 1], device(x, y, to, core))

    def bring_back(d):
        to = around(z, d, NZ)
        return remote(before_out.at[to], before_in.at[z], e2_s.at[d - 1], e2_r.at[d - 1], device(x, y, to, core))

    def apart(k):
        half = lax.div(k + 1, 2)
        return jnp.where(lax.rem(k, 2) == 1, half, -half)

    def owners(g, act):
        @pl.loop(0, NZ // 2)
        def _(k):
            d = lax.rem(NZ // 2 - lax.rem(g + z, 2) + 2 * apart(k), NZ)

            @pl.when(d > 0)
            def _():
                act(d)

    def give_tiles(g):
        all_planes(lambda d: to_plane(g, d).wait_recv())
        state = None
        for i in range(4):
            term = plane[g, i, y] + (plane[g, i, around(y, 1, 4)] + plane[g, i, around(y, 3, 4)])
            state = term if state is None else state + term
            states[i, g] = state
        for t in range(NZ // 2):
            tiles_out[2 * t + g] = states[(3, g) + tile(t)]
        owners(g, lambda d: scatter(d).start())

    def give_before(g):
        @pl.when(lax.rem(z, 2) == g)
        def _():
            tiles_in[z] = tiles_out[z]

            @pl.loop(1, NZ)
            def _(d):
                scatter(d).wait_recv()

            running = jnp.zeros((8, 128), F32)
            for t in range(NZ):
                before_out[t] = running
                running = running + tiles_in[t]

            @pl.loop(0, NZ - 1)
            def _(k):
                bring_back(NZ // 2 + apart(k)).start()

            before_in[z] = before_out[z]

    own_rows = pl.ds(pl.multiple_of(16 * x, 16), 16)

    def to_owner(i, g):
        to = device(2 * lax.div(i, 2) + core, y, z, lax.rem(i, 2))
        here = out.at[0, g, own_rows, :]
        return remote(final.at[i, g], here, f_s.at[4 * g + i], f_r.at[4 * g + x], to)

    def mine(i):
        return jnp.logical_and(x == 2 * lax.div(i, 2) + core, core == lax.rem(i, 2))

    def give_means(g):
        def arrived(d):
            bring_back(NZ - d).wait_recv()

        owners(g, arrived)
        for k in range(4):
            i = lax.rem(2 * (1 - x_hi) + k, 4)
            count = ((4 * z + i + 1) * (LAG_DEV * P_SIZE)).astype(F32)
            for t in range(NZ // 2):
                final[(i, g) + tile(t)] = (before_in[2 * t + g] + states[(i, g) + tile(t)]) / count

            @pl.when(mine(i))
            def _():
                out[0, g, own_rows, :] = final[i, g]

            @pl.when(jnp.logical_not(mine(i)))
            def _():
                to_owner(i, g).start()

            when_drain(jnp.logical_not(mine(i)), functools.partial(to_owner, i, g))

    def take_means(g):
        for i in range(4):
            @pl.when(jnp.logical_not(jnp.logical_and(x == i, core == x_lo)))
            def _():
                here = out.at[0, g, pl.ds(16 * i, 16), :]
                at = 4 * g + i
                remote(final.at[0, g], here, f_s.at[at], f_r.at[at], device(x, y, z, 1 - core)).wait_recv()

    def wait_sent():
        for act in drains:
            act()
        drains.clear()

    for g in (0, 1):
        give_tiles(g)
    wait_sent()
    for g in (0, 1):
        give_before(g)

    @pl.loop(1, NZ)
    def _(d):
        scatter(d).wait_send()

    for g in (0, 1):
        give_means(g)

    @pl.loop(1, NZ)
    def _(d):
        bring_back(d).wait_send()

    for g in (0, 1):
        take_means(g)
    wait_sent()


def body(markov, basis):
    vmem = pl.BlockSpec(memory_space=pltpu.VMEM)
    hbm = pl.BlockSpec(memory_space=pltpu.HBM)
    counts = [15, 15, 24, 24, 24, 24, 8, 8, 2, 2, 4, 4, 30, 30, 15, 15, 15, 15, 8, 8, 2]
    return pl.pallas_call(
        kernel,
        out_shape=jax.ShapeDtypeStruct((1, 2, 64, 512), F32),
        in_specs=[hbm, hbm],
        out_specs=vmem,
        scratch_shapes=[
            pltpu.VMEM((32, 32, 64), F32),
            pltpu.VMEM((16, 32, 128), F32),
            pltpu.VMEM((2, 16, 32, 128), F32),
            pltpu.VMEM((2080, 768), BF16),
            pltpu.VMEM((16, 2, 2, 4, 8, 512), F32),
            pltpu.VMEM((768, 512), BF16),
            pltpu.VMEM((ROWS, 512), F32),
            pltpu.VMEM((ROWS, 512), BF16),
            pltpu.VMEM((ROWS, 512), BF16),
            pltpu.VMEM((512, 1024), BF16),
            pltpu.VMEM((512, 1024), BF16),
            pltpu.VMEM((2, 256, 512), F32),
            pltpu.VMEM((2, 256, 512), F32),
            pltpu.VMEM((2, 256, 512), F32),
            pltpu.VMEM((2, 2, 32, 512), F32),
            pltpu.VMEM((2, 4, 4, 16, 512), F32),
            pltpu.VMEM((4, 2, 16, 512), F32),
            pltpu.VMEM((NZ, 8, 128), F32),
            pltpu.VMEM((NZ, 8, 128), F32),
            pltpu.VMEM((NZ, 8, 128), F32),
            pltpu.VMEM((NZ, 8, 128), F32),
            pltpu.VMEM((4, 2, 16, 512), F32),
        ]
        + [pltpu.SemaphoreType.DMA((2, 4))] * 2
        + [pltpu.SemaphoreType.DMA((n,)) for n in counts],
        compiler_params=pltpu.CompilerParams(
            collective_id=0, has_side_effects=True, vmem_limit_bytes=62 * 1024 * 1024
        ),
        cost_estimate=pl.CostEstimate(flops=10_000_000_000, bytes_accessed=1_000_000, transcendentals=0),
    )(markov, basis)


def solution(mesh):
    placed = (P("lag", "out", None), P("lag", None))
    return jax.shard_map(
        body, mesh=mesh, in_specs=placed, out_specs=P("lag", None, "out", None), check_vma=False
    )
```
